32 devices in a mesh: ctx: 16 (over z, y, x), fsdp: 2 (over core).
Axes of the slice: x: 2, y: 2, z: 4, core: 2. Of those that a mesh axis runs over, the one named last changes fastest.
Arguments:
- hidden_in: bfloat16 [4, 1024, 2048], P('fsdp', 'ctx'), may hold values from -6 to 6
- positions: int32 [1024], replicated, may hold values from 0 to 1023, as said below
- doc_ids: int32 [4, 1024], P('fsdp'), may hold values from 0 to 2, as said below
- norm_attn: bfloat16 [2048], P(('ctx', 'fsdp')), may hold values from 0.25 to 1.75
- w_query: bfloat16 [2048, 2048], P(('ctx', 'fsdp')), may hold values from -0.25 to 0.25
- key_weight: bfloat16 [2048, 256], P(('ctx', 'fsdp')), may hold values from -0.125 to 0.125
- value_weight: bfloat16 [2048, 256], P(('ctx', 'fsdp')), may hold values from -0.125 to 0.125
- w_out: bfloat16 [2048, 2048], P(('ctx', 'fsdp')), may hold values from -0.5 to 0.5
- norm_mlp: bfloat16 [2048], P(('ctx', 'fsdp')), may hold values from 0.25 to 1.75
- w_gate: bfloat16 [2048, 5632], P(('ctx', 'fsdp')), may hold values from -0.125 to 0.125
- w_up: bfloat16 [2048, 5632], P(('ctx', 'fsdp')), may hold values from -0.125 to 0.125
- w_down: bfloat16 [5632, 2048], P(('ctx', 'fsdp')), may hold values from -0.078125 to 0.078125
- cotangent: bfloat16 [4, 1024, 2048], P('fsdp', 'ctx'), may hold values from -6 to 6
Outputs:
- block_out: bfloat16 [4, 1024, 2048], P('fsdp', 'ctx')
- grad_input: float32 [4, 1024, 2048], P('fsdp', 'ctx')
- grad_norm_attn: float32 [2048], P(('ctx', 'fsdp'))
- grad_query: float32 [2048, 2048], P(('ctx', 'fsdp'))
- grad_key: float32 [2048, 256], P(('ctx', 'fsdp'))
- grad_value: float32 [2048, 256], P(('ctx', 'fsdp'))
- grad_out: float32 [2048, 2048], P(('ctx', 'fsdp'))
- grad_norm_mlp: float32 [2048], P(('ctx', 'fsdp'))
- grad_gate: float32 [2048, 5632], P(('ctx', 'fsdp'))
- grad_up: float32 [2048, 5632], P(('ctx', 'fsdp'))
- grad_down: float32 [5632, 2048], P(('ctx', 'fsdp'))
The draws below stay inside these ranges and needn't reach their ends.
Inputs may be any that keep to these rules, and one draw needn't show every extreme that they name: On each device of ctx the 64 rows hold, in order, the positions b * 32 to (b + 1) * 32 - 1 and then 1024 - (b + 1) * 32 to 1024 - b * 32 - 1, for a b of that device's own; the positions are a permutation of 0 to 1023. `doc_ids`: each sequence holds three documents, numbered 0, 1, 2 in the order of their positions; document 0 holds more than half of the 1024 positions, and each document at least one.
All inputs are finite; a program needn't handle non-finite values.
Results may differ from the reference program's by a relative error of at most 0.015.
The reference program's roundings to bfloat16 on the way count: a program that leaves them out, or rounds other values in their place, can miss the bound.
Values may be sent and summed in bfloat16 or wider, within the bound.
No kernel may reach another device: no remote copies, remote signals or barrier semaphores. Data moves between devices by JAX's collectives and lax.ppermute only.
A program may use at most 448 MiB of HBM per device.

```python
import math
import jax
import jax.numpy as jnp
from jax import lax

MODEL_WIDTH = 2048
QUERY_HEADS = 32
KEY_VALUE_HEADS = 4
HEAD_WIDTH = 64
FF = 5632
BLK = 32
LENGTH = 1024
BATCH = 4


def dealt_positions(key):
    pair_count = LENGTH // (2 * BLK)
    pair_choice = jax.random.permutation(key, pair_count).astype(jnp.int32)
    offsets = jnp.arange(BLK, dtype=jnp.int32)
    early_rows = pair_choice[:, None] * BLK + offsets[None, :]
    late_rows = LENGTH - (pair_choice[:, None] + 1) * BLK + offsets[None, :]
    return jnp.concatenate([early_rows, late_rows], axis=1).reshape(LENGTH)


def draw_positions(key, part):
    dealt_rows = dealt_positions(key)
    return dealt_rows.astype(jnp.int32)


def draw_doc_ids(key, part):
    dealt_rows = dealt_positions(key)
    key = jax.random.fold_in(key, 7)
    first_key, second_key = jax.random.split(key)
    first_cut = jax.random.randint(first_key, (BATCH, 1), LENGTH // 2 + 1, LENGTH - 1)
    spread_draw = jax.random.randint(second_key, (BATCH, 1), 0, 1 << 20)
    second_cut = first_cut + 1 + spread_draw % (LENGTH - 1 - first_cut)
    later_first = (dealt_rows[None, :] >= first_cut).astype(jnp.int32)
    later_second = (dealt_rows[None, :] >= second_cut).astype(jnp.int32)
    return (later_first + later_second).astype(jnp.int32)


def block_scale(stream_key, dims, pieces, low, high):
    factor_of, own = 1.0, jax.random.fold_in(stream_key, 6)
    for dim, blocks in pieces:
        heights = jnp.exp(jax.random.uniform(jax.random.fold_in(own, dim), (blocks,), jnp.float32, low / len(pieces), high / len(pieces)))
        factor_of = factor_of * jnp.repeat(heights, dims[dim] // blocks).reshape([-1 if axis == dim else 1 for axis in range(len(dims))])
    return factor_of


def noise(key, dims, scale, reach, shards=(), kind=jnp.bfloat16):
    values = jax.random.normal(key, dims, jnp.float32) * scale
    if len(shards) > 0:
        values = block_scale(key, dims, shards, -0.22, 0.18) * values
    return jnp.clip(values, min=-reach, max=reach).astype(kind)


def setup_inputs(seed: int = 0) -> dict:
    keys = jax.random.split(jax.random.key(seed), 14)
    hidden_in = noise(keys[0], (BATCH, LENGTH, MODEL_WIDTH), 1.0, 6.0, ((0, 2), (1, 16)))
    positions = draw_positions(jax.random.fold_in(keys[13], 71), 0)
    doc_ids = draw_doc_ids(jax.random.fold_in(keys[13], 71), 0)
    norm_attn = jnp.clip(1.0 + 0.15 * jax.random.normal(keys[3], (MODEL_WIDTH,), jnp.float32), 0.25, 1.75).astype(jnp.bfloat16)
    w_query = noise(keys[4], (MODEL_WIDTH, QUERY_HEADS * HEAD_WIDTH), (MODEL_WIDTH // 4) ** -0.5, 0.25, ((0, 32),))
    key_weight = noise(keys[5], (MODEL_WIDTH, KEY_VALUE_HEADS * HEAD_WIDTH), MODEL_WIDTH ** -0.5, 0.125, ((0, 32),))
    value_weight = noise(keys[6], (MODEL_WIDTH, KEY_VALUE_HEADS * HEAD_WIDTH), MODEL_WIDTH ** -0.5, 0.125, ((0, 32),))
    w_out = noise(keys[7], (QUERY_HEADS * HEAD_WIDTH, MODEL_WIDTH), (QUERY_HEADS * HEAD_WIDTH // 16) ** -0.5, 0.5, ((0, 32),))
    norm_mlp = jnp.clip(1.0 + 0.15 * jax.random.normal(keys[8], (MODEL_WIDTH,), jnp.float32), 0.25, 1.75).astype(jnp.bfloat16)
    w_gate = noise(keys[9], (MODEL_WIDTH, FF), MODEL_WIDTH ** -0.5, 0.125, ((0, 32),))
    w_up = noise(keys[10], (MODEL_WIDTH, FF), MODEL_WIDTH ** -0.5, 0.125, ((0, 32),))
    w_down = noise(keys[11], (FF, MODEL_WIDTH), FF ** -0.5, 0.078125, ((0, 32),))
    cotangent = noise(keys[12], (BATCH, LENGTH, MODEL_WIDTH), 1.0, 6.0, ((0, 2), (1, 16)))
    return dict(hidden_in=hidden_in, positions=positions, doc_ids=doc_ids, norm_attn=norm_attn, w_query=w_query, key_weight=key_weight, value_weight=value_weight, w_out=w_out, norm_mlp=norm_mlp, w_gate=w_gate, w_up=w_up, w_down=w_down, cotangent=cotangent)


epsilon = 1e-05
highest = lax.Precision.HIGHEST

@jax.custom_vjp
def lower_bound(v):
    return lax.optimization_barrier(v.astype(jnp.bfloat16)).astype(jnp.float32)

@jax.custom_vjp
def low_back(v):
    return v

def low_keep(v):
    return (lower_bound(v), None)

def low_pass(kept, grad):
    return (grad,)

def back_keep(v):
    return (v, None)

def back_low(kept, grad):
    return (lower_bound(grad),)
lower_bound.defvjp(low_keep, low_pass)
low_back.defvjp(back_keep, back_low)

def rope_tables(positions):
    inverse = 10000.0 ** (-jnp.arange(0, HEAD_WIDTH, 2).astype(jnp.float32) / HEAD_WIDTH)
    angles = positions.astype(jnp.float32)[:, None] * inverse[None, :]
    return (jnp.cos(angles)[:, None, :], jnp.sin(angles)[:, None, :])

def apply_rotation(values, cosine_lookup, sine_lookup):
    half_width = values.shape[-1] // 2
    first_half = values[..., :half_width]
    second_half = values[..., half_width:]
    return jnp.concatenate([first_half * cosine_lookup - second_half * sine_lookup, second_half * cosine_lookup + first_half * sine_lookup], axis=-1)

def rms_norm(values, gain):
    scaling = lax.rsqrt(lax.optimization_barrier(jnp.mean(values * values, axis=-1, keepdims=True)) + epsilon)
    return values * scaling * gain

def attend_block(query_matrix, row_positions, row_docs, key_lookup, value_lookup, positions, doc_rows):
    total_rows = query_matrix.shape[0]
    grouped_heads = query_matrix.reshape(total_rows, KEY_VALUE_HEADS, QUERY_HEADS // KEY_VALUE_HEADS, HEAD_WIDTH)
    scores = jnp.einsum('qngd,knd->ngqk', grouped_heads, key_lookup, precision=highest) * (1.0 / math.sqrt(HEAD_WIDTH))
    scores = low_back(scores)
    visible = (positions[None, :] <= row_positions[:, None]) & (doc_rows[None, :] == row_docs[:, None])
    scores = jnp.where(visible[None, None], scores, -1e+30)
    weights = lower_bound(jax.nn.softmax(scores, axis=-1))
    blended = jnp.einsum('ngqk,knd->qngd', weights, value_lookup, precision=highest)
    return blended.reshape(total_rows, QUERY_HEADS * HEAD_WIDTH)

def sequence_forward(params, sequence, cosine_lookup, sine_lookup, positions, query_block):
    norm_attn, w_query, key_weight, value_weight, w_out, norm_mlp, w_gate, w_up, w_down = params
    hidden, doc_rows = sequence
    token_length = hidden.shape[0]
    normed = lower_bound(rms_norm(hidden, norm_attn))
    proj_query = low_back(jnp.dot(normed, w_query, precision=highest))
    projected_key = low_back(jnp.dot(normed, key_weight, precision=highest))
    projected_value = low_back(jnp.dot(normed, value_weight, precision=highest))
    queries = lower_bound(apply_rotation(proj_query.reshape(token_length, QUERY_HEADS, HEAD_WIDTH), cosine_lookup, sine_lookup))
    key_lookup = lower_bound(apply_rotation(projected_key.reshape(token_length, KEY_VALUE_HEADS, HEAD_WIDTH), cosine_lookup, sine_lookup))
    value_lookup = lower_bound(projected_value).reshape(token_length, KEY_VALUE_HEADS, HEAD_WIDTH)
    blocks = token_length // query_block

    def one_block(block_items):
        query_matrix, row_positions, row_docs = block_items
        return attend_block(query_matrix, row_positions, row_docs, key_lookup, value_lookup, positions, doc_rows)
    blended = lax.map(jax.checkpoint(one_block), (queries.reshape(blocks, query_block, QUERY_HEADS, HEAD_WIDTH), positions.reshape(blocks, query_block), doc_rows.reshape(blocks, query_block)))
    attended = lower_bound(low_back(blended.reshape(token_length, QUERY_HEADS * HEAD_WIDTH)))
    branch = low_back(jnp.dot(attended, w_out, precision=highest))
    middle = hidden + branch
    normed_mlp = lower_bound(rms_norm(middle, norm_mlp))
    gate_proj = low_back(jnp.dot(normed_mlp, w_gate, precision=highest))
    upward = low_back(jnp.dot(normed_mlp, w_up, precision=highest))
    activated = lower_bound(jax.nn.silu(gate_proj) * upward)
    return middle + low_back(jnp.dot(activated, w_down, precision=highest))

def reference(hidden_in, positions, doc_ids, norm_attn, w_query, key_weight, value_weight, w_out, norm_mlp, w_gate, w_up, w_down, cotangent):
    params = tuple((array.astype(jnp.float32) for array in (norm_attn, w_query, key_weight, value_weight, w_out, norm_mlp, w_gate, w_up, w_down)))
    hidden = hidden_in.astype(jnp.float32)
    cosine_lookup, sine_lookup = rope_tables(positions)
    query_block = math.gcd(LENGTH, 512)

    def forward(weights, inputs):

        def one_sequence(sequence):
            return sequence_forward(weights, sequence, cosine_lookup, sine_lookup, positions, query_block)
        return lax.map(jax.checkpoint(one_sequence), (inputs, doc_ids))
    outputs, pullback = jax.vjp(forward, params, hidden)
    grad_params, grad_hidden = pullback(cotangent.astype(jnp.float32))
    return (outputs.astype(jnp.bfloat16), grad_hidden, grad_params[0], grad_params[1], grad_params[2], grad_params[3], grad_params[4], grad_params[5], grad_params[6], grad_params[7], grad_params[8])
```

```python
import functools
import math

import jax
import jax.numpy as jnp
from jax import lax
from jax.experimental import pallas as pl
from jax.experimental.pallas import tpu as pltpu
from jax.sharding import Mesh, PartitionSpec as P

QUERY_HEADS = 32
KEY_VALUE_HEADS = 4
HEAD_WIDTH = 64
GROUP = QUERY_HEADS // KEY_VALUE_HEADS
EPSILON = 1e-05
SCALE = 1.0 / math.sqrt(HEAD_WIDTH)
SWAP = ((0, 1), (1, 0))
CROSS = ((1, 2), (2, 1))
BF16 = jnp.bfloat16
F32 = jnp.float32
VMEM = 56 * 1024 * 1024
COST = pl.CostEstimate(flops=1, bytes_accessed=1, transcendentals=0)

NT = (((1,), (1,)), ((), ()))
TN = (((0,), (0,)), ((), ()))
NN = (((1,), (0,)), ((), ()))


def dot(left, right, dims=NN):
    return lax.dot_general(left, right, dims, preferred_element_type=F32)


def pick(array, index, axis=0):
    return lax.dynamic_index_in_dim(array, index, axis, keepdims=False)


def bit(axis):
    return lax.axis_index(axis)


def swap(array, axis, name="swap"):
    with jax.named_scope(name):
        return lax.ppermute(array, axis, SWAP)


def pair(axis, own, got, at=0):
    first = bit(axis) == 0
    return jnp.stack([jnp.where(first, own, got), jnp.where(first, got, own)], at)


def half_swap(array):
    width = array.shape[-1]
    lane = lax.broadcasted_iota(jnp.int32, array.shape, array.ndim - 1)
    ahead = pltpu.roll(array, width - HEAD_WIDTH // 2, array.ndim - 1)
    behind = pltpu.roll(array, HEAD_WIDTH // 2, array.ndim - 1)
    return jnp.where(lane % HEAD_WIDTH < HEAD_WIDTH // 2, ahead, behind)


def widen(table, width):
    return jnp.concatenate([table] * (width // table.shape[-1]), axis=-1)


def place_of(bits_ref, which):
    high = 1 - bits_ref[0] if which & 1 else bits_ref[0]
    low = 1 - bits_ref[1] if which & 2 else bits_ref[1]
    return high, low


def deal_attn_kernel(queries, kv_of, order, bits_ref, own, far, near, corner, out_ref, scratch):
    rows = own.shape[0]
    columns = out_ref.shape[-1]
    keys = own.shape[1] - 128 - 2 * KEY_VALUE_HEADS * HEAD_WIDTH
    values = keys + KEY_VALUE_HEADS * HEAD_WIDTH
    for which, ref in enumerate((own, far, near, corner)):
        high, low = place_of(bits_ref, which)
        scratch[2 * high + low] = ref[...]
    gains = [scratch[at, :, own.shape[1] - 128 :].astype(F32).T[:16] for at in range(4)]
    gains = jnp.concatenate(gains + [jnp.zeros((16, columns - 4 * rows), F32)], axis=1).astype(BF16)
    for slot, (member, kv) in enumerate(zip(order, kv_of)):
        for at in range(4):
            head = lambda start: scratch[at, :, start + kv * HEAD_WIDTH : start + (kv + 1) * HEAD_WIDTH]
            out_ref[slot, at * rows : (at + 1) * rows, :queries] = scratch[
                at, :, member * queries : (member + 1) * queries
            ]
            if queries < columns - 128:
                out_ref[slot, at * rows : (at + 1) * rows, queries : columns - 128] = jnp.zeros(
                    (rows, columns - 128 - queries), BF16
                )
            both = jnp.concatenate([head(keys), head(values)], axis=1)
            out_ref[slot, at * rows : (at + 1) * rows, columns - 128 :] = both
        out_ref[slot, 4 * rows :] = gains


def deal_attn(bits, order, kv_of, queries, padded, parts):
    rows, width = parts[0].shape
    columns = padded + 128
    shape = (len(order), 4 * rows + 16, columns)
    return pl.pallas_call(
        functools.partial(deal_attn_kernel, queries, kv_of, order),
        in_specs=[pl.BlockSpec(memory_space=pltpu.SMEM)]
        + [pl.BlockSpec(memory_space=pltpu.VMEM)] * 4,
        out_shape=jax.ShapeDtypeStruct(shape, BF16),
        scratch_shapes=[pltpu.VMEM((4, rows, width), BF16)],
        compiler_params=pltpu.CompilerParams(vmem_limit_bytes=VMEM),
        cost_estimate=COST,
        name="deal_attn",
    )(bits, *parts)


def project_kernel(
    x_ref, dealt_ref, cos_ref, sin_ref,
    normed_ref, q_ref, k_ref, v_ref, kt_ref, vt_ref, gains_ref, w_ref,
):
    width = q_ref.shape[-1]
    places, rows = w_ref.shape[1], w_ref.shape[4]

    @pl.when(pl.program_id(0) == 0)
    def _():
        gains = []
        for high in (0, 1):
            for place in range(places):
                for low in (0, 1):
                    for core in (0, 1):
                        at = slice((2 * high + low) * rows, (2 * high + low + 1) * rows)
                        w_ref[high, place, low, core] = dealt_ref[2 * place + core, at, :]
                        both = dealt_ref[2 * place + core, 4 * rows :, at]
                        gains.append(both.astype(F32)[:8])
        gains_ref[...] = jnp.concatenate(gains, axis=1)

    x = x_ref[...].astype(F32)
    r = lax.rsqrt(jnp.mean(x * x, axis=-1, keepdims=True) + EPSILON)
    normed = (x * r * gains_ref[:1, :]).astype(BF16)
    normed_ref[...] = normed
    w = w_ref[...].reshape(x_ref.shape[-1], w_ref.shape[-1])
    y = dot(normed, w)
    q = y[:, :width]
    both = y[:, width:]
    lane = lax.broadcasted_iota(jnp.int32, both.shape, 1)
    other = pltpu.roll(both, HEAD_WIDTH, 1)
    k = jnp.where(lane < HEAD_WIDTH, both, other)
    v = jnp.where(lane < HEAD_WIDTH, other, both)
    turn = lambda a: a * widen(cos_ref[...], a.shape[-1]) + half_swap(a) * widen(sin_ref[...], a.shape[-1])
    q_ref[...] = turn(q).astype(BF16)
    k = widen(turn(k), width)
    v = widen(v, width)
    k_ref[...] = k.astype(BF16)
    v_ref[...] = v.astype(BF16)
    kt_ref[...] = k.T.astype(BF16)
    vt_ref[...] = v.T.astype(BF16)


def project(places, x, dealt, cos, sin):
    rows, width = x.shape
    columns = dealt.shape[2]
    out = columns - 128
    block = 256
    row = lambda n: pl.BlockSpec((block, n), lambda i: (i, 0))
    across = pl.BlockSpec((out, block), lambda i: (0, i))
    shape = jax.ShapeDtypeStruct
    whole = (2, places, 2, 2, (dealt.shape[1] - 16) // 4, columns)
    return pl.pallas_call(
        project_kernel,
        grid=(rows // block,),
        in_specs=[row(width), pl.BlockSpec(dealt.shape, lambda i: (0, 0, 0)), row(128), row(128)],
        out_specs=[row(width), row(out), row(out), row(out), across, across]
        + [pl.BlockSpec((8, width), lambda i: (0, 0))]
        + [pl.BlockSpec(whole, lambda i: (0, 0, 0, 0, 0, 0))],
        out_shape=[shape((rows, n), BF16) for n in (width, out, out, out)]
        + [shape((out, rows), BF16)] * 2
        + [shape((8, width), F32), shape(whole, BF16)],
        compiler_params=pltpu.CompilerParams(vmem_limit_bytes=VMEM),
        cost_estimate=COST,
        name="project",
    )(x, dealt, cos, sin)


def forward_kernel(heads, q_ref, k_ref, vt_ref, pq_ref, dq_ref, pk_ref, dk_ref, out_ref, lse_ref):
    q = q_ref[...]
    visible = (pk_ref[...] <= pq_ref[...]) & (dk_ref[...] == dq_ref[...])
    lane = lax.broadcasted_iota(jnp.int32, q.shape, 1) // HEAD_WIDTH
    wide = (q.shape[1], q.shape[0])
    row = lax.broadcasted_iota(jnp.int32, wide, 0) // HEAD_WIDTH
    total = jnp.zeros(wide, F32)
    lse_ref[...] = jnp.zeros_like(lse_ref)
    for head in range(heads):
        own = jnp.where(lane == head, q, jnp.zeros_like(q))
        scores = jnp.where(visible, dot(k_ref[...], own, NT) * SCALE, -1e30)
        top = jnp.max(scores, axis=0, keepdims=True)
        powers = jnp.exp(scores - top)
        mass = jnp.sum(powers, axis=0, keepdims=True)
        lse_ref[head : head + 1, :] = top + jnp.log(mass)
        chances = (powers * (1.0 / mass)).astype(BF16)
        total = jnp.where(row == head, dot(vt_ref[...], chances), total)
    out_ref[...] = total.T.astype(BF16)


def query_block(rows):
    return 256 if rows <= 1024 else 128


def attend_forward(heads, q, k, vt, positions, docs):
    rows, width = q.shape
    block = query_block(rows)
    row = pl.BlockSpec((block, width), lambda i: (i, 0))
    across = pl.BlockSpec((1, block), lambda i: (0, i))
    whole = lambda a: pl.BlockSpec(a.shape, lambda i: (0, 0))
    down = (positions[:, None], docs[:, None])
    flat = (positions[None], docs[None])
    return pl.pallas_call(
        functools.partial(forward_kernel, heads),
        grid=(rows // block,),
        in_specs=[row, whole(k), whole(vt), across, across, whole(down[0]), whole(down[1])],
        out_specs=[row, pl.BlockSpec((8, block), lambda i: (0, i))],
        out_shape=[
            jax.ShapeDtypeStruct((rows, width), BF16),
            jax.ShapeDtypeStruct((8, rows), F32),
        ],
        compiler_params=pltpu.CompilerParams(vmem_limit_bytes=VMEM),
        cost_estimate=COST,
        name="attend_forward",
    )(q, k, vt, *flat, *down)


def backward_kernel(
    heads, q_ref, g_ref, k_ref, v_ref, kt_ref, pq_ref, dq_ref, pk_ref, dk_ref, lse_ref,
    cos_ref, sin_ref, cos_all_ref, sin_all_ref, gq_ref, gkv_ref, gk_sum, gv_sum,
):
    step = pl.program_id(0)

    @pl.when(step == 0)
    def _():
        gk_sum[...] = jnp.zeros_like(gk_sum)
        gv_sum[...] = jnp.zeros_like(gv_sum)

    q = q_ref[...]
    g = g_ref[...]
    visible = (pk_ref[...] <= pq_ref[...]) & (dk_ref[...] == dq_ref[...])
    lane = lax.broadcasted_iota(jnp.int32, q.shape, 1) // HEAD_WIDTH
    wide = (q.shape[1], q.shape[0])
    row = lax.broadcasted_iota(jnp.int32, wide, 0) // HEAD_WIDTH
    total = jnp.zeros(wide, F32)
    for head in range(heads):
        own = jnp.where(lane == head, q, jnp.zeros_like(q))
        own_g = jnp.where(lane == head, g, jnp.zeros_like(g))
        scores = dot(k_ref[...], own, NT) * SCALE
        chances = jnp.where(visible, jnp.exp(scores - lse_ref[head : head + 1, :]), 0.0)
        grads = dot(v_ref[...], own_g, NT)
        inner = jnp.sum(chances * grads, axis=0, keepdims=True)
        grad_scores = (chances * (grads - inner)).astype(BF16)
        gv_sum[...] += dot(chances.astype(BF16), own_g)
        gk_sum[...] += dot(grad_scores, own)
        total = jnp.where(row == head, dot(kt_ref[...], grad_scores), total)
    gq = total.T * SCALE
    width = gq.shape[-1]
    gq = gq * widen(cos_ref[...], width) - half_swap(gq) * widen(sin_ref[...], width)
    gq_ref[...] = gq.astype(BF16)

    @pl.when(step == pl.num_programs(0) - 1)
    def _():
        def fold(array):
            parts = [array[:, at : at + 128] for at in range(0, array.shape[-1], 128)]
            both = functools.reduce(lambda a, b: a + b, parts)
            return both + pltpu.roll(both, HEAD_WIDTH, 1)

        gk = fold(gk_sum[...]) * SCALE
        gk = gk * cos_all_ref[...] - half_swap(gk) * sin_all_ref[...]
        gv = fold(gv_sum[...])
        lane = lax.broadcasted_iota(jnp.int32, gk.shape, 1)
        gkv_ref[...] = jnp.where(lane < HEAD_WIDTH, gk, gv).astype(BF16)


def attend_backward(heads, q, g, k, v, kt, positions, docs, lse, cos, sin):
    rows, width = q.shape
    block = query_block(rows)
    row = lambda n: pl.BlockSpec((block, n), lambda i: (i, 0))
    across = lambda n: pl.BlockSpec((n, block), lambda i: (0, i))
    whole = lambda a: pl.BlockSpec(a.shape, lambda i: (0, 0))
    down = (positions[:, None], docs[:, None])
    flat = (positions[None], docs[None])
    return pl.pallas_call(
        functools.partial(backward_kernel, heads),
        grid=(rows // block,),
        in_specs=[
            row(width), row(width), whole(k), whole(v), whole(kt), across(1), across(1),
            whole(down[0]), whole(down[1]), across(8), row(128), row(128), whole(cos), whole(sin),
        ],
        out_specs=[row(width), pl.BlockSpec((rows, 128), lambda i: (0, 0))],
        out_shape=[
            jax.ShapeDtypeStruct((rows, width), BF16),
            jax.ShapeDtypeStruct((rows, 128), BF16),
        ],
        scratch_shapes=[pltpu.VMEM((rows, width), F32), pltpu.VMEM((rows, width), F32)],
        compiler_params=pltpu.CompilerParams(vmem_limit_bytes=VMEM),
        cost_estimate=COST,
        name="attend_backward",
    )(q, g, k, v, kt, *flat, *down, lse, cos, sin, cos, sin)


def feed_kernel(bits_ref, n_ref, g_ref, down_ref, *refs):
    parts = refs[:8]
    act_ref, back_ref, w_ref, sem = refs[8:]

    @pl.when(pl.program_id(0) == 0)
    def _():
        copies = []
        for at, part in enumerate(parts):
            which, chunk = at % 4, at // 4
            high, low = place_of(bits_ref, which)
            size = part.shape[0]
            places = pl.ds(chunk * size, size)
            copies.append(
                pltpu.make_async_copy(part, w_ref.at[high, places, low], sem.at[at])
            )
        for copy in copies:
            copy.start()
        for copy in copies:
            copy.wait()

    units = act_ref.shape[-1]
    both = dot(n_ref[...], w_ref[...].reshape(n_ref.shape[-1], 2 * units))
    gate, up = both[:, :units], both[:, units:]
    grad = dot(g_ref[...], down_ref[...], NT)
    s = jax.nn.sigmoid(gate)
    silu = gate * s
    act_ref[...] = (silu * up).astype(BF16)
    back = jnp.concatenate([grad * up * s * (1.0 + gate * (1.0 - s)), grad * silu], axis=1)
    back_ref[...] = back.astype(BF16)


def feed_forward(bits, n, g, down, parts):
    rows, width = n.shape
    places, piece, columns = parts[0].shape
    units = columns // 2
    block = 256
    row = lambda w: pl.BlockSpec((block, w), lambda i: (i, 0))
    whole = (2, 2 * places, 2, piece, columns)
    return pl.pallas_call(
        feed_kernel,
        grid=(rows // block,),
        in_specs=[
            pl.BlockSpec(memory_space=pltpu.SMEM),
            row(width),
            row(width),
            pl.BlockSpec(down.shape, lambda i: (0, 0)),
        ]
        + [pl.BlockSpec(memory_space=pl.ANY)] * 8,
        out_specs=[row(units), row(columns), pl.BlockSpec(whole, lambda i: (0, 0, 0, 0, 0))],
        out_shape=[
            jax.ShapeDtypeStruct((rows, units), BF16),
            jax.ShapeDtypeStruct((rows, columns), BF16),
            jax.ShapeDtypeStruct(whole, BF16),
        ],
        scratch_shapes=[pltpu.SemaphoreType.DMA((8,))],
        compiler_params=pltpu.CompilerParams(vmem_limit_bytes=VMEM),
        cost_estimate=COST,
        name="feed_forward",
    )(bits, n, g, down, *parts)


def rows_kernel(sides, chunks, bits_ref, left_ref, right_ref, *refs):
    outs, scratch = refs[:-1], refs[-1]
    step, chunk = pl.program_id(0), pl.program_id(1)
    low = bits_ref[1]
    scratch[...] = dot(left_ref[...], right_ref[...], TN).astype(BF16)
    for side in range(len(sides)):
        for part in range(chunks):

            @pl.when((step == side) & (chunk == part))
            def _():
                for beside in (0, 1):
                    out = outs[(side * 2 + beside) * chunks + part]
                    rows = out.shape[1]
                    column = 1 - low if beside else low
                    for place in range(out.shape[0]):
                        start = pl.multiple_of((2 * place + column) * rows, rows)
                        out[place] = scratch[pl.ds(start, rows), :]


def outer_rows(sides, chunks, places, bits, left, right):
    rows, width = left.shape
    columns = right.shape[1]
    piece = width // (4 * places)
    block = width // (2 * chunks)
    shape = (places // chunks, piece, columns)
    count = len(sides) * 2 * chunks
    first = sides[0]
    outs = pl.pallas_call(
        functools.partial(rows_kernel, sides, chunks),
        grid_spec=pltpu.PrefetchScalarGridSpec(
            num_scalar_prefetch=1,
            grid=(len(sides), chunks),
            in_specs=[
                pl.BlockSpec(
                    (rows, block),
                    lambda i, j, bits: (0, jnp.bitwise_xor(bits[0], jnp.bitwise_xor(i, first)) * chunks + j),
                ),
                pl.BlockSpec(right.shape, lambda i, j, bits: (0, 0)),
            ],
            out_specs=[pl.BlockSpec(shape, lambda i, j, bits: (0, 0, 0))] * count,
            scratch_shapes=[pltpu.VMEM((block, columns), BF16)],
        ),
        out_shape=[jax.ShapeDtypeStruct(shape, BF16)] * count,
        compiler_params=pltpu.CompilerParams(vmem_limit_bytes=VMEM),
        cost_estimate=COST,
        name="outer_rows",
    )(bits, left, right)
    return [list(outs[at : at + chunks]) for at in range(0, count, chunks)]


def quarters_kernel(flip, bits_ref, left_ref, right_ref, own, near, theirs, far, scratch):
    scratch[...] = dot(left_ref[...], right_ref[...], TN).astype(BF16)
    rows = own.shape[0]
    for ref, there, beside in ((own, 0, 0), (near, 0, 1), (theirs, 1, 0), (far, 1, 1)):
        high = 1 - bits_ref[0] if there else bits_ref[0]
        low = 1 - bits_ref[1] if beside else bits_ref[1]
        at = 2 * low + high if flip else 2 * high + low
        ref[...] = scratch[pl.ds(pl.multiple_of(at * rows, rows), rows), :]


def outer_quarters(flip, bits, left, right):
    rows, width = left.shape
    columns = right.shape[1]
    block = min(columns, 512)
    piece = width // 4
    if piece % 16:
        product = dot(left, right, TN).astype(BF16).reshape(2, 2, piece, columns)
        high, low = (bits[1], bits[0]) if flip else (bits[0], bits[1])
        sides = ((0, 0), (1, 0), (0, 1), (1, 1)) if flip else ((0, 0), (0, 1), (1, 0), (1, 1))
        return [pick(pick(product, high ^ a), low ^ b) for a, b in sides]
    return pl.pallas_call(
        functools.partial(quarters_kernel, flip),
        grid_spec=pltpu.PrefetchScalarGridSpec(
            num_scalar_prefetch=1,
            grid=(columns // block,),
            in_specs=[
                pl.BlockSpec(left.shape, lambda i, bits: (0, 0)),
                pl.BlockSpec((rows, block), lambda i, bits: (0, i)),
            ],
            out_specs=[pl.BlockSpec((piece, block), lambda i, bits: (0, i))] * 4,
            scratch_shapes=[pltpu.VMEM((width, block), BF16)],
        ),
        out_shape=[jax.ShapeDtypeStruct((piece, columns), BF16)] * 4,
        compiler_params=pltpu.CompilerParams(vmem_limit_bytes=VMEM),
        cost_estimate=COST,
        name="outer_quarters",
    )(bits, left, right)


def deal_kernel(places, gate_ref, up_ref, out_ref):
    rows, columns = gate_ref.shape
    piece = columns // (8 * places)
    for place in range(places):
        for core in (0, 1):
            starts = [
                (((high * places + place) * 2 + low) * 2 + core) * piece
                for high in (0, 1)
                for low in (0, 1)
            ]
            out_ref[2 * place + core] = jnp.concatenate(
                [ref[:, start : start + piece] for ref in (gate_ref, up_ref) for start in starts],
                axis=1,
            )


def deal(places, gate, up):
    rows, columns = gate.shape
    return pl.pallas_call(
        functools.partial(deal_kernel, places),
        out_shape=jax.ShapeDtypeStruct((2 * places, rows, columns // places), BF16),
        compiler_params=pltpu.CompilerParams(vmem_limit_bytes=VMEM),
        cost_estimate=COST,
        name="deal",
    )(gate, up)


def collect_kernel(places, in_ref, gate_ref, up_ref):
    rows, columns = gate_ref.shape
    piece = columns // (8 * places)
    for which, ref in enumerate((gate_ref, up_ref)):
        pieces = []
        for high in (0, 1):
            for place in range(places):
                for low in (0, 1):
                    for core in (0, 1):
                        start = (4 * which + 2 * high + low) * piece
                        got = in_ref[2 * place + core][:, start : start + piece]
                        pieces.append(got.astype(F32))
        ref[...] = jnp.concatenate(pieces, axis=1)


def collect(places, array):
    _, rows, columns = array.shape
    shape = jax.ShapeDtypeStruct((rows, places * columns), F32)
    return pl.pallas_call(
        functools.partial(collect_kernel, places),
        out_shape=[shape, shape],
        compiler_params=pltpu.CompilerParams(vmem_limit_bytes=VMEM),
        cost_estimate=COST,
        name="collect",
    )(array)


def sum_kernel(count, *refs):
    outs = refs[3 * count + 1 :]
    for at in range(count):
        own, near, relayed = refs[3 * at : 3 * at + 3]
        total = own[...].astype(F32) + near[...].astype(F32) + relayed[...].astype(F32)
        outs[at][...] = total.astype(outs[at].dtype)


def sum_parts(dtype, after, *groups):
    vmem = pl.BlockSpec(memory_space=pltpu.VMEM)
    return pl.pallas_call(
        functools.partial(sum_kernel, len(groups)),
        in_specs=[vmem] * (3 * len(groups)) + [pl.BlockSpec(memory_space=pl.ANY)],
        out_shape=[jax.ShapeDtypeStruct(group[0].shape, dtype) for group in groups],
        compiler_params=pltpu.CompilerParams(vmem_limit_bytes=VMEM),
        cost_estimate=COST,
        name="sum_parts",
    )(*[part for group in groups for part in group], after)


def rope_tables(positions):
    inverse = 10000.0 ** (-jnp.arange(0, HEAD_WIDTH, 2).astype(F32) / HEAD_WIDTH)
    angles = positions.astype(F32)[:, None] * inverse[None, :]
    cos, sin = jnp.cos(angles), jnp.sin(angles)
    return jnp.concatenate([cos] * 4, 1), jnp.concatenate([-sin, sin] * 2, 1)


def norm_back(upstream, values, gain):
    scaling = lax.rsqrt(jnp.mean(values * values, axis=-1, keepdims=True) + EPSILON)
    scaled_grad = upstream * gain
    return scaling * scaled_grad - values * (scaling * scaling * scaling) * jnp.mean(
        scaled_grad * values, axis=-1, keepdims=True
    )


class Layout:
    def __init__(self, mesh):
        bits = mesh.shape["ctx"].bit_length() - 1
        self.ctx = tuple(f"p{i}" for i in range(bits))
        self.mesh = Mesh(
            mesh.devices.reshape((2,) * bits + (mesh.shape["fsdp"],)), self.ctx + ("core",)
        )
        self.high, self.low = self.ctx[0], self.ctx[-1]
        self.mid = self.ctx[1:-1]
        self.places = 2 ** len(self.mid)
        self.members = 2 * self.places
        self.all = self.ctx + ("core",)
        self.turn = [
            [(4 * h + 2 * l + c, 4 * c + 2 * (l ^ other) + h) for h in (0, 1) for l in (0, 1) for c in (0, 1)]
            for other in (0, 1)
        ]

    def cross(self, array):
        got = lax.ppermute(array, (self.high, "core"), CROSS)
        return jnp.where(bit(self.high) == bit("core"), array, got)

    def turned(self, array, other, name):
        with jax.named_scope(name):
            return lax.ppermute(array, (self.high, self.low, "core"), self.turn[other])

    def to_team(self, array, name):
        low = bit(self.low)
        return self.turned(pick(array, low), 0, name), self.turned(pick(array, 1 - low), 1, name)

    def in_order(self, blocks):
        both = pair(self.low, *blocks)
        return both.reshape(-1, both.shape[-1])

    def from_team(self, array, name):
        low = bit(self.low)
        both = array.reshape(2, -1, array.shape[-1])
        return pair(
            self.low,
            self.turned(pick(both, low), 0, name),
            self.turned(pick(both, 1 - low), 1, name),
        )

    def team_gather(self, array):
        return lax.all_gather(array, ("core",) + self.mid, axis=0, tiled=True)


    def scatter_cores(self, rows_of, then=None):
        core = bit("core")
        sent = rows_of(1 - core).astype(BF16)
        got = swap(sent, "core", "sum_cores")
        if then is not None:
            then(sent)
        mine = rows_of(core) + got.astype(F32)
        width = mine.shape[1]
        mine = mine.astype(BF16).reshape((2,) * len(self.mid) + (-1, width))
        return [mine[..., : width // 2], mine[..., width // 2 :]]

    def scatter_send(self, parts, count):
        pending = []
        for part, order in zip(parts, (list(self.mid), list(self.mid[::-1]))):
            left = [axis for axis in self.mid if axis not in order[:count]]
            at = left.index(order[count])
            there = bit(order[count])
            pending.append((pick(part, there, at), swap(pick(part, 1 - there, at), order[count], f"sum_places_{count}")))
        return pending

    def scatter_add(self, pending):
        last = pending[0][0].ndim == 2
        parts = [own.astype(F32) + got.astype(F32) for own, got in pending]
        return jnp.concatenate(parts, 1) if last else [part.astype(BF16) for part in parts]

    def scatter_rows(self, rows_of, then=()):
        then = list(then) + [lambda parts: parts] * (1 + len(self.mid) - len(then))
        parts = self.scatter_cores(rows_of, then[0])
        for count in range(len(self.mid)):
            parts = self.scatter_add(self.scatter_send(then[1 + count](parts), count))
        return parts

    def exchange(self, array):
        return lax.all_to_all(array, self.mid + ("core",), 0, 0, tiled=True)

    def rows_out(self, array):
        shape = array.shape
        return jnp.swapaxes(array.reshape((2, self.places) + shape[1:]), 0, 1).reshape(shape)

    def rows_in(self, array):
        shape = array.shape
        return jnp.swapaxes(array.reshape((self.places, 2) + shape[1:]), 0, 1).reshape(shape)


    def start_four(self, array, name):
        return swap(array, self.high, name + "_far"), swap(array, self.low, name + "_near")

    def corner_four(self, far, name):
        return swap(far, self.low, name + "_corner")

    def join_four(self, first, second, own, far, near, corner):
        return pair(first, pair(second, own, near), pair(second, far, corner))

    def relay_sum(self, theirs, got_far, name):
        relay = theirs.astype(F32) + got_far.astype(F32)
        return swap(relay.astype(BF16), self.high, name + "_relay")


def shards(
    layout,
    hidden_in,
    positions,
    doc_ids,
    norm_attn,
    w_query,
    key_weight,
    value_weight,
    w_out,
    norm_mlp,
    w_gate,
    w_up,
    w_down,
    cotangent,
):
    members, places = layout.members, layout.places
    width = hidden_in.shape[-1]
    weight_rows = w_query.shape[0]
    heads = QUERY_HEADS // members
    padded = max(heads, 2)
    query_width = heads * HEAD_WIDTH
    padding = (padded - heads) * HEAD_WIDTH
    tie = lax.optimization_barrier
    place = sum(bit(axis) * 2**at for at, axis in enumerate(layout.mid[::-1]))
    bits = jnp.stack([bit(layout.high), bit(layout.low), 2 * place + bit("core")])
    bits = bits.astype(jnp.int32)
    order = [core * places + place for place in range(places) for core in (0, 1)]
    kv_of = [member * heads // GROUP for member in order]


    blocks = layout.to_team(hidden_in, "hidden")
    docs = layout.cross(pick(doc_ids, bit(layout.low)))
    gains = jnp.stack([norm_attn, norm_mlp], axis=1)
    gains = jnp.pad(gains, ((0, 0), (0, 126)))
    raw = jnp.concatenate([w_query, key_weight, value_weight, gains], axis=1)
    raw_far, raw_near = layout.start_four(raw, "raw")
    x = layout.in_order(blocks)
    x_team = layout.team_gather(x)
    cos, sin = rope_tables(positions)
    dealt = deal(places, w_gate, w_up)
    raw_far, raw_near, w_out, down_sent, cotangent, cos, sin, positions, docs, dealt = tie(
        (raw_far, raw_near, w_out, w_down, cotangent, cos, sin, positions, docs, dealt)
    )
    raw_corner = layout.corner_four(raw_far, "raw")
    out_part = layout.cross(w_out)
    g_blocks = layout.to_team(cotangent, "cotangent")
    dealt_attn = deal_attn(
        bits, order, kv_of, query_width, query_width + padding, (raw, raw_far, raw_near, raw_corner)
    )
    dealt_attn, out_part, down_sent, *g_blocks = tie((dealt_attn, out_part, down_sent, *g_blocks))
    dealt_attn = layout.exchange(dealt_attn)
    out_far, out_near = layout.start_four(out_part, "out")
    down_far, down_near = layout.start_four(down_sent, "down")
    g_rows = layout.in_order(g_blocks)
    g = layout.team_gather(g_rows)
    dealt_attn, out_far, out_near, dealt = tie((dealt_attn, out_far, out_near, dealt))
    dealt = layout.exchange(dealt)
    out_corner = layout.corner_four(out_far, "out")

    normed_attn, q, k, v, kt, vt, gains, w_attn = project(places, x_team, dealt_attn, cos, sin)
    gain_attn, gain_mlp = gains[:1], gains[1:2]
    q, out_corner, down_far, down_near = tie((q, out_corner, down_far, down_near))
    down_corner = layout.corner_four(down_far, "down")
    attended, lse = attend_forward(heads, q, k, vt, positions, docs)
    attended, dealt, down_corner = tie((attended, dealt, down_corner))
    dealt = dealt.reshape(places, 2 * weight_rows, -1)
    chunk = lambda a, at: a[at * places // 2 : (at + 1) * places // 2]
    gu_parts = [chunk(dealt, 0), chunk(dealt, 1)]
    gu_far, gu_near, gu_corner = [None] * 2, [None] * 2, [None] * 2
    gu_far[0], gu_near[0] = layout.start_four(gu_parts[0], "gate_up_0")
    out_own = layout.join_four(layout.low, layout.high, out_part, out_near, out_far, out_corner)
    out_own = out_own.reshape(query_width, width)
    down_own = layout.join_four(
        layout.high, layout.low, w_down, down_far, down_near, down_corner
    ).reshape(-1, width)
    attended = attended[:, :query_width]

    half = x_team.shape[0] // 2
    part = lambda a, core: lax.dynamic_slice_in_dim(a, core * half, half, 0)
    same = lambda parts: parts
    late = {}

    def weights_on(parts):
        *parts, gu_far[0], gu_near[0], gu_parts[1] = tie(
            (*parts, gu_far[0], gu_near[0], gu_parts[1])
        )
        gu_corner[0] = layout.corner_four(gu_far[0], "gate_up_0")
        gu_far[1], gu_near[1] = layout.start_four(gu_parts[1], "gate_up_1")
        return parts

    branch = layout.scatter_rows(
        lambda core: dot(part(attended, core), out_own), (None, same, weights_on)
    )
    x_wide = x.astype(F32)
    middle = x_wide + branch
    scale_mlp = lax.rsqrt(jnp.mean(middle * middle, axis=-1, keepdims=True) + EPSILON)
    normed_mlp = layout.team_gather((middle * scale_mlp * gain_mlp).astype(BF16))
    gu_corner[1] = layout.corner_four(gu_far[1], "gate_up_1")

    activated, grad_gu, w_gu = feed_forward(
        bits,
        normed_mlp,
        g,
        down_own,
        [
            parts[at]
            for at in range(2)
            for parts in (gu_parts, gu_far, gu_near, gu_corner)
        ],
    )
    w_gu = w_gu.reshape(width, -1)

    down_parts = outer_quarters(False, bits, activated, g)
    grad_gu, activated, down_parts = tie((grad_gu, activated, down_parts))
    down_far = swap(down_parts[3], layout.low, "grad_down_far")

    def gu_terms(parts):
        *parts, right = tie((*parts, grad_gu))
        late["theirs"], late["far"] = outer_rows((1,), 2, places, bits, normed_mlp, right)
        return parts

    def gu_others(parts):
        *parts, late["far"], late["theirs"], right, late["down_far"] = tie(
            (*parts, late["far"], late["theirs"], grad_gu, down_far)
        )
        late["far"][0] = swap(late["far"][0], layout.low, "grad_gate_up_far_0")
        late["down_relay"] = layout.relay_sum(down_parts[2], late["down_far"], "grad_down")
        late["own"], late["near"] = outer_rows((0,), 2, places, bits, normed_mlp, right)
        return parts

    grad_normed_mlp = layout.scatter_rows(
        lambda core: dot(part(grad_gu, core), w_gu, NT), (None, gu_terms, gu_others)
    )
    gu_theirs, gu_far, gu_own, gu_near = (late[key] for key in ("theirs", "far", "own", "near"))
    down_relay = late["down_relay"]
    grad_normed_mlp, gu_own, gu_near = tie((grad_normed_mlp, gu_own, gu_near))
    grad_middle = g_rows.astype(F32) + norm_back(grad_normed_mlp, middle, gain_mlp)
    grad_branch = grad_middle.astype(BF16)
    branch_team = layout.team_gather(grad_branch)
    gu_far[0], act, grad_branch, sent = tie((gu_far[0], activated, grad_branch, gu_far[1]))
    gu_far[1] = swap(sent, layout.low, "grad_gate_up_far_1")
    gu_relay = [layout.relay_sum(gu_theirs[0], gu_far[0], "grad_gate_up_0")]
    final = layout.scatter_cores(lambda core: dot(part(act, core), down_own))
    branch_team, gu_far[1], down_sent, near_sent, *final = tie(
        (branch_team, gu_far[1], down_parts[1], gu_near[0], *final)
    )
    gu_relay.append(layout.relay_sum(gu_theirs[1], gu_far[1], "grad_gate_up_1"))
    down_near = swap(down_sent, layout.low, "grad_down_near")
    final = layout.scatter_send(final, 0)
    grad_attended = dot(branch_team, out_own, NT).astype(BF16)
    if padding:
        grad_attended = jnp.pad(grad_attended, ((0, 0), (0, padding)))

    gq, gkv = attend_backward(heads, q, grad_attended, k, v, kt, positions, docs, lse, cos, sin)
    grad_qkv = jnp.concatenate([gq, gkv], axis=1)
    grad_qkv, final, down_near, near_sent = tie((grad_qkv, final, down_near, near_sent))
    gu_near[0] = swap(near_sent, layout.low, "grad_gate_up_near_0")
    for count in range(1, len(layout.mid)):
        final = layout.scatter_send(layout.scatter_add(final), count)

    w_attn_own = w_attn.reshape(width, -1)[:, : grad_qkv.shape[1]]

    def attn_terms(sent):
        _, right = tie((sent, grad_qkv))
        late["attn"] = [part for (part,) in outer_rows((1, 0), 1, places, bits, normed_attn, right)]
        late["attn_far"] = swap(late["attn"][1], layout.low, "grad_attn_far")

    def out_terms(parts):
        *parts, late["attn"], right, late["final"] = tie(
            (*parts, late["attn"], branch_team, final)
        )
        late["out"] = outer_quarters(True, bits, attended, right)
        return parts

    def relays_on(parts):
        *parts, late["attn_far"], late["out"], gu_near[0], sent, gu_relay[0] = tie(
            (*parts, late["attn_far"], late["out"], gu_near[0], gu_near[1], gu_relay[0])
        )
        gu_near[1] = swap(sent, layout.low, "grad_gate_up_near_1")
        late["out_far"] = swap(late["out"][3], layout.low, "grad_out_far")
        return parts

    grad_normed_attn = layout.scatter_rows(
        lambda core: dot(part(grad_qkv, core), w_attn_own, NT), (attn_terms, out_terms, relays_on)
    )
    attn_parts, out_parts = late["attn"], late["out"]
    grad_normed_attn, final, out_far, attn_far, attn_sent = tie(
        (grad_normed_attn, late["final"], late["out_far"], late["attn_far"], attn_parts[3])
    )
    attn_relay = layout.relay_sum(attn_parts[0], attn_far, "grad_attn")
    attn_near = swap(attn_sent, layout.low, "grad_attn_near")
    final = layout.scatter_add(final)
    block_out = layout.from_team((middle + final).astype(BF16), "block_out")
    out_relay = layout.relay_sum(out_parts[2], out_far, "grad_out")
    out_near = swap(out_parts[1], layout.low, "grad_out_near")
    grad_input = grad_middle + norm_back(grad_normed_attn, x_wide, gain_attn)
    grad_rows = grad_input.astype(BF16)
    grad_input = layout.from_team(grad_rows, "grad_input").astype(F32)

    by_member = lambda a: a.reshape(members, weight_rows, -1)
    dealt = sum_parts(BF16, grad_rows, *zip(gu_own, gu_near, gu_relay))
    dealt = layout.exchange(by_member(jnp.concatenate(dealt)))
    (grad_attn,) = sum_parts(BF16, grad_rows, (attn_parts[2], attn_near, attn_relay))
    grad_attn = layout.rows_in(layout.exchange(by_member(grad_attn))).astype(F32)
    (grad_out,) = sum_parts(BF16, grad_rows, (out_parts[0], out_near, out_relay))
    grad_out = layout.cross(grad_out).astype(F32)
    (grad_down,) = sum_parts(F32, grad_rows, (down_parts[0], down_near, down_relay))
    grad_gate, grad_up = collect(places, dealt)

    def sum_kv(array):
        return array.reshape((KEY_VALUE_HEADS, -1) + array.shape[1:]).sum(1)

    def lay(array):
        return jnp.swapaxes(array, 0, 1).reshape(array.shape[1], -1)

    grad_query = lay(grad_attn[:, :, :query_width])
    grad_kv = sum_kv(grad_attn[:, :, query_width + padding :])
    grad_key = lay(grad_kv[:, :, :HEAD_WIDTH])
    grad_value = lay(grad_kv[:, :, HEAD_WIDTH:])

    def gain_gradient(gain, *terms):
        total = sum(jnp.sum(w.astype(F32) * grad, axis=1) for w, grad in terms)
        return total / gain.astype(F32)

    grad_norm_attn = gain_gradient(
        norm_attn, (w_query, grad_query), (key_weight, grad_key), (value_weight, grad_value)
    )
    grad_norm_mlp = gain_gradient(norm_mlp, (w_gate, grad_gate), (w_up, grad_up))

    return (
        block_out,
        grad_input,
        grad_norm_attn,
        grad_query,
        grad_key,
        grad_value,
        grad_out,
        grad_norm_mlp,
        grad_gate,
        grad_up,
        grad_down,
    )


def solution(mesh):
    layout = Layout(mesh)
    tokens = P("core", layout.ctx, None)
    rows = P(layout.all, None)
    line = P(layout.all)
    in_specs = (
        tokens, P(), P("core", None), line, rows, rows, rows, rows, line, rows, rows, rows, tokens,
    )
    out_specs = (tokens, tokens, line, rows, rows, rows, rows, line, rows, rows, rows)
    return jax.shard_map(
        functools.partial(shards, layout),
        mesh=layout.mesh,
        in_specs=in_specs,
        out_specs=out_specs,
        check_vma=False,
    )
```

```python
import functools
import math

import jax
import jax.numpy as jnp
from jax import lax
from jax.experimental import pallas as pl
from jax.experimental.pallas import tpu as pltpu
from jax.sharding import Mesh, PartitionSpec as P

QUERY_HEADS = 32
KEY_VALUE_HEADS = 4
HEAD_WIDTH = 64
GROUP = QUERY_HEADS // KEY_VALUE_HEADS
EPSILON = 1e-05
SCALE = 1.0 / math.sqrt(HEAD_WIDTH)
SWAP = ((0, 1), (1, 0))
CROSS = ((1, 2), (2, 1))
BF16 = jnp.bfloat16
F32 = jnp.float32
VMEM = 32 * 1024 * 1024
COST = pl.CostEstimate(flops=1, bytes_accessed=1, transcendentals=0)

NT = (((1,), (1,)), ((), ()))
TN = (((0,), (0,)), ((), ()))
NN = (((1,), (0,)), ((), ()))


def dot(left, right, dims=NN):
    return lax.dot_general(left, right, dims, preferred_element_type=F32)


def pick(array, index, axis=0):
    return lax.dynamic_index_in_dim(array, index, axis, keepdims=False)


def bit(axis):
    return lax.axis_index(axis)


def swap(array, axis, name="swap"):
    with jax.named_scope(name):
        return lax.ppermute(array, axis, SWAP)


def pair(axis, own, got, at=0):
    first = bit(axis) == 0
    return jnp.stack([jnp.where(first, own, got), jnp.where(first, got, own)], at)


def half_swap(array):
    width = array.shape[-1]
    lane = lax.broadcasted_iota(jnp.int32, array.shape, array.ndim - 1)
    ahead = pltpu.roll(array, width - HEAD_WIDTH // 2, array.ndim - 1)
    behind = pltpu.roll(array, HEAD_WIDTH // 2, array.ndim - 1)
    return jnp.where(lane % HEAD_WIDTH < HEAD_WIDTH // 2, ahead, behind)


def widen(table, width):
    return jnp.concatenate([table] * (width // table.shape[-1]), axis=-1)


def place_of(bits_ref, which):
    high = 1 - bits_ref[0] if which & 1 else bits_ref[0]
    low = 1 - bits_ref[1] if which & 2 else bits_ref[1]
    return high, low


def deal_attn_kernel(queries, kv_of, order, bits_ref, own, far, near, corner, out_ref, scratch):
    rows = own.shape[0]
    columns = out_ref.shape[-1]
    keys = own.shape[1] - 128 - 2 * KEY_VALUE_HEADS * HEAD_WIDTH
    values = keys + KEY_VALUE_HEADS * HEAD_WIDTH
    for which, ref in enumerate((own, far, near, corner)):
        high, low = place_of(bits_ref, which)
        scratch[2 * high + low] = ref[...]
    gains = [scratch[at, :, own.shape[1] - 128 :].astype(F32).T[:16] for at in range(4)]
    gains = jnp.concatenate(gains + [jnp.zeros((16, columns - 4 * rows), F32)], axis=1).astype(BF16)
    for slot, (member, kv) in enumerate(zip(order, kv_of)):
        for at in range(4):
            head = lambda start: scratch[at, :, start + kv * HEAD_WIDTH : start + (kv + 1) * HEAD_WIDTH]
            out_ref[slot, at * rows : (at + 1) * rows, :queries] = scratch[
                at, :, member * queries : (member + 1) * queries
            ]
            if queries < columns - 128:
                out_ref[slot, at * rows : (at + 1) * rows, queries : columns - 128] = jnp.zeros(
                    (rows, columns - 128 - queries), BF16
                )
            both = jnp.concatenate([head(keys), head(values)], axis=1)
            out_ref[slot, at * rows : (at + 1) * rows, columns - 128 :] = both
        out_ref[slot, 4 * rows :] = gains


def deal_attn(bits, order, kv_of, queries, padded, parts):
    rows, width = parts[0].shape
    columns = padded + 128
    shape = (len(order), 4 * rows + 16, columns)
    return pl.pallas_call(
        functools.partial(deal_attn_kernel, queries, kv_of, order),
        in_specs=[pl.BlockSpec(memory_space=pltpu.SMEM)]
        + [pl.BlockSpec(memory_space=pltpu.VMEM)] * 4,
        out_shape=jax.ShapeDtypeStruct(shape, BF16),
        scratch_shapes=[pltpu.VMEM((4, rows, width), BF16)],
        compiler_params=pltpu.CompilerParams(vmem_limit_bytes=VMEM),
        cost_estimate=COST,
        name="deal_attn",
    )(bits, *parts)


def project_kernel(
    x_ref, dealt_ref, cos_ref, sin_ref,
    normed_ref, q_ref, k_ref, v_ref, kt_ref, vt_ref, gains_ref, w_ref,
):
    width = q_ref.shape[-1]
    places, rows = w_ref.shape[1], w_ref.shape[4]

    @pl.when(pl.program_id(0) == 0)
    def _():
        gains = []
        for high in (0, 1):
            for place in range(places):
                for low in (0, 1):
                    for core in (0, 1):
                        at = slice((2 * high + low) * rows, (2 * high + low + 1) * rows)
                        w_ref[high, place, low, core] = dealt_ref[2 * place + core, at, :]
                        both = dealt_ref[2 * place + core, 4 * rows :, at]
                        gains.append(both.astype(F32)[:8])
        gains_ref[...] = jnp.concatenate(gains, axis=1)

    x = x_ref[...].astype(F32)
    r = lax.rsqrt(jnp.mean(x * x, axis=-1, keepdims=True) + EPSILON)
    normed = (x * r * gains_ref[:1, :]).astype(BF16)
    normed_ref[...] = normed
    w = w_ref[...].reshape(x_ref.shape[-1], w_ref.shape[-1])
    y = dot(normed, w)
    q = y[:, :width]
    both = y[:, width:]
    lane = lax.broadcasted_iota(jnp.int32, both.shape, 1)
    other = pltpu.roll(both, HEAD_WIDTH, 1)
    k = jnp.where(lane < HEAD_WIDTH, both, other)
    v = jnp.where(lane < HEAD_WIDTH, other, both)
    turn = lambda a: a * widen(cos_ref[...], a.shape[-1]) + half_swap(a) * widen(sin_ref[...], a.shape[-1])
    q_ref[...] = turn(q).astype(BF16)
    k = widen(turn(k), width)
    v = widen(v, width)
    k_ref[...] = k.astype(BF16)
    v_ref[...] = v.astype(BF16)
    kt_ref[...] = k.T.astype(BF16)
    vt_ref[...] = v.T.astype(BF16)


def project(places, x, dealt, cos, sin):
    rows, width = x.shape
    columns = dealt.shape[2]
    out = columns - 128
    block = 256
    row = lambda n: pl.BlockSpec((block, n), lambda i: (i, 0))
    across = pl.BlockSpec((out, block), lambda i: (0, i))
    shape = jax.ShapeDtypeStruct
    whole = (2, places, 2, 2, (dealt.shape[1] - 16) // 4, columns)
    return pl.pallas_call(
        project_kernel,
        grid=(rows // block,),
        in_specs=[row(width), pl.BlockSpec(dealt.shape, lambda i: (0, 0, 0)), row(128), row(128)],
        out_specs=[row(width), row(out), row(out), row(out), across, across]
        + [pl.BlockSpec((8, width), lambda i: (0, 0))]
        + [pl.BlockSpec(whole, lambda i: (0, 0, 0, 0, 0, 0))],
        out_shape=[shape((rows, n), BF16) for n in (width, out, out, out)]
        + [shape((out, rows), BF16)] * 2
        + [shape((8, width), F32), shape(whole, BF16)],
        compiler_params=pltpu.CompilerParams(vmem_limit_bytes=VMEM),
        cost_estimate=COST,
        name="project",
    )(x, dealt, cos, sin)


def visible_to(marks_all, marks):
    marks = marks.T
    return (marks_all[:, :1] <= marks[:1, :]) & (marks_all[:, 1:2] == marks[1:2, :])


def forward_kernel(heads, q_ref, k_ref, vt_ref, marks_ref, marks_all_ref, out_ref, lse_ref):
    q = q_ref[...]
    visible = visible_to(marks_all_ref[...], marks_ref[...])
    lane = lax.broadcasted_iota(jnp.int32, q.shape, 1) // HEAD_WIDTH
    wide = (q.shape[1], q.shape[0])
    row = lax.broadcasted_iota(jnp.int32, wide, 0) // HEAD_WIDTH
    total = jnp.zeros(wide, F32)
    lse_ref[...] = jnp.zeros_like(lse_ref)
    for head in range(heads):
        own = jnp.where(lane == head, q, jnp.zeros_like(q))
        scores = jnp.where(visible, dot(k_ref[...], own, NT) * SCALE, -1e30)
        top = jnp.max(scores, axis=0, keepdims=True)
        powers = jnp.exp(scores - top)
        mass = jnp.sum(powers, axis=0, keepdims=True)
        lse_ref[head : head + 1, :] = top + jnp.log(mass)
        chances = (powers * (1.0 / mass)).astype(BF16)
        total = jnp.where(row == head, dot(vt_ref[...], chances), total)
    out_ref[...] = total.T.astype(BF16)


def query_block(rows):
    return 256 if rows <= 1024 else 128


def attend_forward(heads, q, k, vt, marks):
    rows, width = q.shape
    block = query_block(rows)
    row = pl.BlockSpec((block, width), lambda i: (i, 0))
    mark = pl.BlockSpec((block, 128), lambda i: (i, 0))
    whole = lambda a: pl.BlockSpec(a.shape, lambda i: (0, 0))
    return pl.pallas_call(
        functools.partial(forward_kernel, heads),
        grid=(rows // block,),
        in_specs=[row, whole(k), whole(vt), mark, whole(marks)],
        out_specs=[row, pl.BlockSpec((8, block), lambda i: (0, i))],
        out_shape=[
            jax.ShapeDtypeStruct((rows, width), BF16),
            jax.ShapeDtypeStruct((8, rows), F32),
        ],
        compiler_params=pltpu.CompilerParams(vmem_limit_bytes=VMEM),
        cost_estimate=COST,
        name="attend_forward",
    )(q, k, vt, marks, marks)


def backward_kernel(
    heads, q_ref, g_ref, k_ref, v_ref, kt_ref, marks_ref, marks_all_ref, lse_ref,
    cos_ref, sin_ref, cos_all_ref, sin_all_ref, gq_ref, gkv_ref, gk_sum, gv_sum,
):
    step = pl.program_id(0)

    @pl.when(step == 0)
    def _():
        gk_sum[...] = jnp.zeros_like(gk_sum)
        gv_sum[...] = jnp.zeros_like(gv_sum)

    q = q_ref[...]
    g = g_ref[...]
    visible = visible_to(marks_all_ref[...], marks_ref[...])
    lane = lax.broadcasted_iota(jnp.int32, q.shape, 1) // HEAD_WIDTH
    wide = (q.shape[1], q.shape[0])
    row = lax.broadcasted_iota(jnp.int32, wide, 0) // HEAD_WIDTH
    total = jnp.zeros(wide, F32)
    for head in range(heads):
        own = jnp.where(lane == head, q, jnp.zeros_like(q))
        own_g = jnp.where(lane == head, g, jnp.zeros_like(g))
        scores = dot(k_ref[...], own, NT) * SCALE
        chances = jnp.where(visible, jnp.exp(scores - lse_ref[head : head + 1, :]), 0.0)
        grads = dot(v_ref[...], own_g, NT)
        inner = jnp.sum(chances * grads, axis=0, keepdims=True)
        grad_scores = (chances * (grads - inner)).astype(BF16)
        gv_sum[...] += dot(chances.astype(BF16), own_g)
        gk_sum[...] += dot(grad_scores, own)
        total = jnp.where(row == head, dot(kt_ref[...], grad_scores), total)
    gq = total.T * SCALE
    width = gq.shape[-1]
    gq = gq * widen(cos_ref[...], width) - half_swap(gq) * widen(sin_ref[...], width)
    gq_ref[...] = gq.astype(BF16)

    @pl.when(step == pl.num_programs(0) - 1)
    def _():
        def fold(array):
            parts = [array[:, at : at + 128] for at in range(0, array.shape[-1], 128)]
            both = functools.reduce(lambda a, b: a + b, parts)
            return both + pltpu.roll(both, HEAD_WIDTH, 1)

        gk = fold(gk_sum[...]) * SCALE
        gk = gk * cos_all_ref[...] - half_swap(gk) * sin_all_ref[...]
        gv = fold(gv_sum[...])
        lane = lax.broadcasted_iota(jnp.int32, gk.shape, 1)
        gkv_ref[...] = jnp.where(lane < HEAD_WIDTH, gk, gv).astype(BF16)


def attend_backward(heads, q, g, k, v, kt, marks, lse, cos, sin):
    rows, width = q.shape
    block = query_block(rows)
    row = lambda n: pl.BlockSpec((block, n), lambda i: (i, 0))
    across = lambda n: pl.BlockSpec((n, block), lambda i: (0, i))
    whole = lambda a: pl.BlockSpec(a.shape, lambda i: (0, 0))
    return pl.pallas_call(
        functools.partial(backward_kernel, heads),
        grid=(rows // block,),
        in_specs=[
            row(width), row(width), whole(k), whole(v), whole(kt), row(128), whole(marks),
            across(8), row(128), row(128), whole(cos), whole(sin),
        ],
        out_specs=[row(width), pl.BlockSpec((rows, 128), lambda i: (0, 0))],
        out_shape=[
            jax.ShapeDtypeStruct((rows, width), BF16),
            jax.ShapeDtypeStruct((rows, 128), BF16),
        ],
        scratch_shapes=[pltpu.VMEM((rows, width), F32), pltpu.VMEM((rows, width), F32)],
        compiler_params=pltpu.CompilerParams(vmem_limit_bytes=VMEM),
        cost_estimate=COST,
        name="attend_backward",
    )(q, g, k, v, kt, marks, marks, lse, cos, sin, cos, sin)


def feed_kernel(bits_ref, n_ref, g_ref, down_ref, *refs):
    parts = refs[:8]
    act_ref, back_ref, w_ref, sem = refs[8:]

    @pl.when(pl.program_id(0) == 0)
    def _():
        copies = []
        for at, part in enumerate(parts):
            which, chunk = at % 4, at // 4
            high, low = place_of(bits_ref, which)
            size = part.shape[0]
            places = pl.ds(chunk * size, size)
            copies.append(
                pltpu.make_async_copy(part, w_ref.at[high, places, low], sem.at[at])
            )
        for copy in copies:
            copy.start()
        for copy in copies:
            copy.wait()

    units = act_ref.shape[-1]
    both = dot(n_ref[...], w_ref[...].reshape(n_ref.shape[-1], 2 * units))
    gate, up = both[:, :units], both[:, units:]
    grad = dot(g_ref[...], down_ref[...], NT)
    s = jax.nn.sigmoid(gate)
    silu = gate * s
    act_ref[...] = (silu * up).astype(BF16)
    back = jnp.concatenate([grad * up * s * (1.0 + gate * (1.0 - s)), grad * silu], axis=1)
    back_ref[...] = back.astype(BF16)


def feed_forward(bits, n, g, down, parts):
    rows, width = n.shape
    places, piece, columns = parts[0].shape
    units = columns // 2
    block = 256
    row = lambda w: pl.BlockSpec((block, w), lambda i: (i, 0))
    whole = (2, 2 * places, 2, piece, columns)
    return pl.pallas_call(
        feed_kernel,
        grid=(rows // block,),
        in_specs=[
            pl.BlockSpec(memory_space=pltpu.SMEM),
            row(width),
            row(width),
            pl.BlockSpec(down.shape, lambda i: (0, 0)),
        ]
        + [pl.BlockSpec(memory_space=pl.ANY)] * 8,
        out_specs=[row(units), row(columns), pl.BlockSpec(whole, lambda i: (0, 0, 0, 0, 0))],
        out_shape=[
            jax.ShapeDtypeStruct((rows, units), BF16),
            jax.ShapeDtypeStruct((rows, columns), BF16),
            jax.ShapeDtypeStruct(whole, BF16),
        ],
        scratch_shapes=[pltpu.SemaphoreType.DMA((8,))],
        compiler_params=pltpu.CompilerParams(vmem_limit_bytes=VMEM),
        cost_estimate=COST,
        name="feed_forward",
    )(bits, n, g, down, *parts)


def rows_kernel(sides, chunks, bits_ref, left_ref, right_ref, *refs):
    outs, scratch = refs[:-1], refs[-1]
    step, chunk = pl.program_id(0), pl.program_id(1)
    low = bits_ref[1]
    scratch[...] = dot(left_ref[...], right_ref[...], TN).astype(BF16)
    for side in range(len(sides)):
        for part in range(chunks):

            @pl.when((step == side) & (chunk == part))
            def _():
                for beside in (0, 1):
                    out = outs[(side * 2 + beside) * chunks + part]
                    rows = out.shape[1]
                    column = 1 - low if beside else low
                    for place in range(out.shape[0]):
                        start = pl.multiple_of((2 * place + column) * rows, rows)
                        out[place] = scratch[pl.ds(start, rows), :]


def outer_rows(sides, chunks, places, bits, left, right):
    rows, width = left.shape
    columns = right.shape[1]
    piece = width // (4 * places)
    block = width // (2 * chunks)
    shape = (places // chunks, piece, columns)
    count = len(sides) * 2 * chunks
    first = sides[0]
    outs = pl.pallas_call(
        functools.partial(rows_kernel, sides, chunks),
        grid_spec=pltpu.PrefetchScalarGridSpec(
            num_scalar_prefetch=1,
            grid=(len(sides), chunks),
            in_specs=[
                pl.BlockSpec(
                    (rows, block),
                    lambda i, j, bits: (0, jnp.bitwise_xor(bits[0], jnp.bitwise_xor(i, first)) * chunks + j),
                ),
                pl.BlockSpec(right.shape, lambda i, j, bits: (0, 0)),
            ],
            out_specs=[pl.BlockSpec(shape, lambda i, j, bits: (0, 0, 0))] * count,
            scratch_shapes=[pltpu.VMEM((block, columns), BF16)],
        ),
        out_shape=[jax.ShapeDtypeStruct(shape, BF16)] * count,
        compiler_params=pltpu.CompilerParams(vmem_limit_bytes=VMEM),
        cost_estimate=COST,
        name="outer_rows",
    )(bits, left, right)
    return [list(outs[at : at + chunks]) for at in range(0, count, chunks)]


def quarters_kernel(flip, bits_ref, left_ref, right_ref, own, near, theirs, far, scratch):
    scratch[...] = dot(left_ref[...], right_ref[...], TN).astype(BF16)
    rows = own.shape[0]
    for ref, there, beside in ((own, 0, 0), (near, 0, 1), (theirs, 1, 0), (far, 1, 1)):
        high = 1 - bits_ref[0] if there else bits_ref[0]
        low = 1 - bits_ref[1] if beside else bits_ref[1]
        at = 2 * low + high if flip else 2 * high + low
        ref[...] = scratch[pl.ds(pl.multiple_of(at * rows, rows), rows), :]


def outer_quarters(flip, bits, left, right):
    rows, width = left.shape
    columns = right.shape[1]
    block = min(columns, 512)
    piece = width // 4
    if piece % 16:
        product = dot(left, right, TN).astype(BF16).reshape(2, 2, piece, columns)
        high, low = (bits[1], bits[0]) if flip else (bits[0], bits[1])
        sides = ((0, 0), (1, 0), (0, 1), (1, 1)) if flip else ((0, 0), (0, 1), (1, 0), (1, 1))
        return [pick(pick(product, high ^ a), low ^ b) for a, b in sides]
    return pl.pallas_call(
        functools.partial(quarters_kernel, flip),
        grid_spec=pltpu.PrefetchScalarGridSpec(
            num_scalar_prefetch=1,
            grid=(columns // block,),
            in_specs=[
                pl.BlockSpec(left.shape, lambda i, bits: (0, 0)),
                pl.BlockSpec((rows, block), lambda i, bits: (0, i)),
            ],
            out_specs=[pl.BlockSpec((piece, block), lambda i, bits: (0, i))] * 4,
            scratch_shapes=[pltpu.VMEM((width, block), BF16)],
        ),
        out_shape=[jax.ShapeDtypeStruct((piece, columns), BF16)] * 4,
        compiler_params=pltpu.CompilerParams(vmem_limit_bytes=VMEM),
        cost_estimate=COST,
        name="outer_quarters",
    )(bits, left, right)


def deal_kernel(places, gate_ref, up_ref, out_ref):
    rows, columns = gate_ref.shape
    piece = columns // (8 * places)
    for place in range(places):
        for core in (0, 1):
            starts = [
                (((high * places + place) * 2 + low) * 2 + core) * piece
                for high in (0, 1)
                for low in (0, 1)
            ]
            out_ref[2 * place + core] = jnp.concatenate(
                [ref[:, start : start + piece] for ref in (gate_ref, up_ref) for start in starts],
                axis=1,
            )


def deal(places, gate, up):
    rows, columns = gate.shape
    return pl.pallas_call(
        functools.partial(deal_kernel, places),
        out_shape=jax.ShapeDtypeStruct((2 * places, rows, columns // places), BF16),
        compiler_params=pltpu.CompilerParams(vmem_limit_bytes=VMEM),
        cost_estimate=COST,
        name="deal",
    )(gate, up)


def collect_kernel(places, in_ref, gate_ref, up_ref):
    rows, columns = gate_ref.shape
    piece = columns // (8 * places)
    for which, ref in enumerate((gate_ref, up_ref)):
        pieces = []
        for high in (0, 1):
            for place in range(places):
                for low in (0, 1):
                    for core in (0, 1):
                        start = (4 * which + 2 * high + low) * piece
                        got = in_ref[2 * place + core][:, start : start + piece]
                        pieces.append(got.astype(F32))
        ref[...] = jnp.concatenate(pieces, axis=1)


def collect(places, array):
    _, rows, columns = array.shape
    shape = jax.ShapeDtypeStruct((rows, places * columns), F32)
    return pl.pallas_call(
        functools.partial(collect_kernel, places),
        out_shape=[shape, shape],
        compiler_params=pltpu.CompilerParams(vmem_limit_bytes=VMEM),
        cost_estimate=COST,
        name="collect",
    )(array)


def sum_kernel(count, *refs):
    outs = refs[-count:]
    for at in range(count):
        own, near, relayed = refs[3 * at : 3 * at + 3]
        total = own[...].astype(F32) + near[...].astype(F32) + relayed[...].astype(F32)
        outs[at][...] = total.astype(outs[at].dtype)


def sum_parts(dtype, after, *groups):
    vmem = pl.BlockSpec(memory_space=pltpu.VMEM)
    return pl.pallas_call(
        functools.partial(sum_kernel, len(groups)),
        in_specs=[vmem] * (3 * len(groups)) + [pl.BlockSpec(memory_space=pl.ANY)] * len(after),
        out_shape=[jax.ShapeDtypeStruct(group[0].shape, dtype) for group in groups],
        compiler_params=pltpu.CompilerParams(vmem_limit_bytes=VMEM),
        cost_estimate=COST,
        name="sum_parts",
    )(*[part for group in groups for part in group], *after)


def row_tables(positions, docs):
    inverse = 10000.0 ** (-jnp.arange(0, HEAD_WIDTH, 2).astype(F32) / HEAD_WIDTH)
    angles = positions.astype(F32)[:, None] * inverse[None, :]
    cos, sin = jnp.cos(angles), jnp.sin(angles)
    marks = jnp.stack([positions, docs], axis=1).astype(F32)
    marks = jnp.pad(marks, ((0, 0), (0, 126)))
    return jnp.concatenate([cos] * 4, 1), jnp.concatenate([-sin, sin] * 2, 1), marks


def norm_back(upstream, values, gain):
    scaling = lax.rsqrt(jnp.mean(values * values, axis=-1, keepdims=True) + EPSILON)
    scaled_grad = upstream * gain
    return scaling * scaled_grad - values * (scaling * scaling * scaling) * jnp.mean(
        scaled_grad * values, axis=-1, keepdims=True
    )


class Layout:
    def __init__(self, mesh):
        bits = mesh.shape["ctx"].bit_length() - 1
        self.ctx = tuple(f"p{i}" for i in range(bits))
        self.mesh = Mesh(
            mesh.devices.reshape((2,) * bits + (mesh.shape["fsdp"],)), self.ctx + ("core",)
        )
        self.high, self.low = self.ctx[0], self.ctx[-1]
        self.mid = self.ctx[1:-1]
        self.places = 2 ** len(self.mid)
        self.members = 2 * self.places
        self.all = self.ctx + ("core",)
        self.turn = [
            [(4 * h + 2 * l + c, 4 * c + 2 * (l ^ other) + h) for h in (0, 1) for l in (0, 1) for c in (0, 1)]
            for other in (0, 1)
        ]

    def cross(self, array):
        got = lax.ppermute(array, (self.high, "core"), CROSS)
        return jnp.where(bit(self.high) == bit("core"), array, got)

    def turned(self, array, other, name):
        with jax.named_scope(name):
            return lax.ppermute(array, (self.high, self.low, "core"), self.turn[other])

    def to_team(self, array, name):
        low = bit(self.low)
        return self.turned(pick(array, low), 0, name), self.turned(pick(array, 1 - low), 1, name)

    def in_order(self, blocks):
        both = pair(self.low, *blocks)
        return both.reshape(-1, both.shape[-1])

    def from_team(self, array, name):
        low = bit(self.low)
        both = array.reshape(2, -1, array.shape[-1])
        return pair(
            self.low,
            self.turned(pick(both, low), 0, name),
            self.turned(pick(both, 1 - low), 1, name),
        )

    def team_gather(self, array):
        return lax.all_gather(array, ("core",) + self.mid, axis=0, tiled=True)


    def scatter_cores(self, rows_of, then=None):
        core = bit("core")
        sent = rows_of(1 - core).astype(BF16)
        got = swap(sent, "core", "sum_cores")
        if then is not None:
            then(sent)
        mine = rows_of(core) + got.astype(F32)
        width = mine.shape[1]
        mine = mine.astype(BF16).reshape((2,) * len(self.mid) + (-1, width))
        return [mine[..., : width // 2], mine[..., width // 2 :]]

    def scatter_send(self, parts, count):
        pending = []
        for part, order in zip(parts, (list(self.mid), list(self.mid[::-1]))):
            left = [axis for axis in self.mid if axis not in order[:count]]
            at = left.index(order[count])
            there = bit(order[count])
            pending.append((pick(part, there, at), swap(pick(part, 1 - there, at), order[count], f"sum_places_{count}")))
        return pending

    def scatter_add(self, pending):
        last = pending[0][0].ndim == 2
        parts = [own.astype(F32) + got.astype(F32) for own, got in pending]
        return jnp.concatenate(parts, 1) if last else [part.astype(BF16) for part in parts]

    def scatter_rows(self, rows_of, then=()):
        then = list(then) + [lambda parts: parts] * (1 + len(self.mid) - len(then))
        parts = self.scatter_cores(rows_of, then[0])
        for count in range(len(self.mid)):
            parts = self.scatter_add(self.scatter_send(then[1 + count](parts), count))
        return parts

    def exchange(self, array):
        return lax.all_to_all(array, self.mid + ("core",), 0, 0, tiled=True)

    def rows_out(self, array):
        shape = array.shape
        return jnp.swapaxes(array.reshape((2, self.places) + shape[1:]), 0, 1).reshape(shape)

    def rows_in(self, array):
        shape = array.shape
        return jnp.swapaxes(array.reshape((self.places, 2) + shape[1:]), 0, 1).reshape(shape)


    def start_four(self, array, name):
        return swap(array, self.high, name + "_far"), swap(array, self.low, name + "_near")

    def corner_four(self, far, name):
        return swap(far, self.low, name + "_corner")

    def join_four(self, first, second, own, far, near, corner):
        return pair(first, pair(second, own, near), pair(second, far, corner))

    def relay_sum(self, theirs, got_far, name):
        relay = theirs.astype(F32) + got_far.astype(F32)
        return swap(relay.astype(BF16), self.high, name + "_relay")


def shards(
    layout,
    hidden_in,
    positions,
    doc_ids,
    norm_attn,
    w_query,
    key_weight,
    value_weight,
    w_out,
    norm_mlp,
    w_gate,
    w_up,
    w_down,
    cotangent,
):
    members, places = layout.members, layout.places
    width = hidden_in.shape[-1]
    weight_rows = w_query.shape[0]
    heads = QUERY_HEADS // members
    padded = max(heads, 2)
    query_width = heads * HEAD_WIDTH
    padding = (padded - heads) * HEAD_WIDTH
    tie = lax.optimization_barrier
    place = sum(bit(axis) * 2**at for at, axis in enumerate(layout.mid[::-1]))
    bits = jnp.stack([bit(layout.high), bit(layout.low), 2 * place + bit("core")])
    bits = bits.astype(jnp.int32)
    order = [core * places + place for place in range(places) for core in (0, 1)]
    kv_of = [member * heads // GROUP for member in order]


    blocks = layout.to_team(hidden_in, "hidden")
    docs = layout.cross(pick(doc_ids, bit(layout.low)))
    gains = jnp.stack([norm_attn, norm_mlp], axis=1)
    gains = jnp.pad(gains, ((0, 0), (0, 126)))
    raw = jnp.concatenate([w_query, key_weight, value_weight, gains], axis=1)
    raw_far, raw_near = layout.start_four(raw, "raw")
    x = layout.in_order(blocks)
    x_team = layout.team_gather(x)
    cos, sin, marks = row_tables(positions, docs)
    dealt = deal(places, w_gate, w_up)
    raw_far, raw_near, w_out, cotangent, cos, sin, marks, dealt = tie(
        (raw_far, raw_near, w_out, cotangent, cos, sin, marks, dealt)
    )
    raw_corner = layout.corner_four(raw_far, "raw")
    out_part = layout.cross(w_out)
    g_blocks = layout.to_team(cotangent, "cotangent")
    dealt_attn = deal_attn(
        bits, order, kv_of, query_width, query_width + padding, (raw, raw_far, raw_near, raw_corner)
    )
    dealt_attn, out_part, w_down, *g_blocks = tie((dealt_attn, out_part, w_down, *g_blocks))
    dealt_attn = layout.exchange(dealt_attn)
    down_own = lax.all_gather(w_down, (layout.high, layout.low), axis=0, tiled=True)
    out_far, out_near = layout.start_four(out_part, "out")
    g_rows = layout.in_order(g_blocks)
    g = layout.team_gather(g_rows)
    dealt_attn, out_far, out_near, dealt = tie((dealt_attn, out_far, out_near, dealt))
    dealt = layout.exchange(dealt)
    out_corner = layout.corner_four(out_far, "out")

    normed_attn, q, k, v, kt, vt, gains, w_attn = project(places, x_team, dealt_attn, cos, sin)
    gain_attn, gain_mlp = gains[:1], gains[1:2]
    attended, lse = attend_forward(heads, q, k, vt, marks)
    attended, out_corner, dealt = tie((attended, out_corner, dealt))
    dealt = dealt.reshape(places, 2 * weight_rows, -1)
    chunk = lambda a, at: a[at * places // 2 : (at + 1) * places // 2]
    gu_parts = [chunk(dealt, 0), chunk(dealt, 1)]
    gu_far, gu_near, gu_corner = [None] * 2, [None] * 2, [None] * 2
    gu_far[0], gu_near[0] = layout.start_four(gu_parts[0], "gate_up_0")
    out_own = layout.join_four(layout.low, layout.high, out_part, out_near, out_far, out_corner)
    out_own = out_own.reshape(query_width, width)
    attended = attended[:, :query_width]

    half = x_team.shape[0] // 2
    part = lambda a, core: lax.dynamic_slice_in_dim(a, core * half, half, 0)
    same = lambda parts: parts
    late = {}

    def weights_on(parts):
        *parts, gu_far[0], gu_near[0], gu_parts[1] = tie(
            (*parts, gu_far[0], gu_near[0], gu_parts[1])
        )
        gu_corner[0] = layout.corner_four(gu_far[0], "gate_up_0")
        gu_far[1], gu_near[1] = layout.start_four(gu_parts[1], "gate_up_1")
        return parts

    branch = layout.scatter_rows(lambda core: dot(part(attended, core), out_own))
    (branch,) = weights_on((branch,))
    x_wide = x.astype(F32)
    middle = x_wide + branch
    scale_mlp = lax.rsqrt(jnp.mean(middle * middle, axis=-1, keepdims=True) + EPSILON)
    normed_mlp = layout.team_gather((middle * scale_mlp * gain_mlp).astype(BF16))
    gu_corner[1] = layout.corner_four(gu_far[1], "gate_up_1")

    activated, grad_gu, w_gu = feed_forward(
        bits,
        normed_mlp,
        g,
        down_own,
        [
            parts[at]
            for at in range(2)
            for parts in (gu_parts, gu_far, gu_near, gu_corner)
        ],
    )
    w_gu = w_gu.reshape(width, -1)

    def gu_terms(parts):
        *parts, right = tie((*parts, grad_gu))
        late["theirs"], late["far"] = outer_rows((1,), 2, places, bits, normed_mlp, right)
        return parts

    def gu_others(parts):
        *parts, late["far"], late["theirs"], right = tie(
            (*parts, late["far"], late["theirs"], grad_gu)
        )
        late["far"][0] = swap(late["far"][0], layout.low, "grad_gate_up_far_0")
        late["own"], late["near"] = outer_rows((0,), 2, places, bits, normed_mlp, right)
        return parts

    grad_normed_mlp = layout.scatter_rows(
        lambda core: dot(part(grad_gu, core), w_gu, NT), (None, gu_terms, gu_others)
    )
    gu_theirs, gu_far, gu_own, gu_near = (late[key] for key in ("theirs", "far", "own", "near"))
    grad_normed_mlp, gu_own, gu_near, gu_far[0] = tie((grad_normed_mlp, gu_own, gu_near, gu_far[0]))
    grad_middle = g_rows.astype(F32) + norm_back(grad_normed_mlp, middle, gain_mlp)
    grad_branch = grad_middle.astype(BF16)
    branch_team = layout.team_gather(grad_branch)
    gu_far[0], act, grad_branch, sent = tie((gu_far[0], activated, grad_branch, gu_far[1]))
    gu_relay = [layout.relay_sum(gu_theirs[0], gu_far[0], "grad_gate_up_0")]
    gu_far[1] = swap(sent, layout.low, "grad_gate_up_far_1")
    grad_down = dot(act, g, TN).astype(BF16)
    act, grad_down = tie((act, grad_down))
    final = layout.scatter_cores(lambda core: dot(part(act, core), down_own))
    branch_team, grad_down, gu_far[1], gu_relay[0], gu_near, *final = tie(
        (branch_team, grad_down, gu_far[1], gu_relay[0], gu_near, *final)
    )
    gu_relay.append(layout.relay_sum(gu_theirs[1], gu_far[1], "grad_gate_up_1"))
    gu_near = [swap(near, layout.low, f"grad_gate_up_near_{at}") for at, near in enumerate(gu_near)]
    grad_down = lax.psum_scatter(
        grad_down, (layout.high, layout.low), scatter_dimension=0, tiled=True
    ).astype(F32)
    final = layout.scatter_send(final, 0)
    grad_attended = dot(branch_team, out_own, NT).astype(BF16)
    if padding:
        grad_attended = jnp.pad(grad_attended, ((0, 0), (0, padding)))

    gq, gkv = attend_backward(heads, q, grad_attended, k, v, kt, marks, lse, cos, sin)
    grad_qkv = jnp.concatenate([gq, gkv], axis=1)
    grad_qkv, final, gu_near, gu_relay[1] = tie((grad_qkv, final, gu_near, gu_relay[1]))
    for count in range(1, len(layout.mid)):
        final = layout.scatter_send(layout.scatter_add(final), count)

    w_attn_own = w_attn.reshape(width, -1)[:, : grad_qkv.shape[1]]

    def attn_terms(sent):
        _, right = tie((sent, grad_qkv))
        late["attn"] = [part for (part,) in outer_rows((1, 0), 1, places, bits, normed_attn, right)]
        late["attn_far"] = swap(late["attn"][1], layout.low, "grad_attn_far")

    def out_terms(parts):
        *parts, late["attn"], right, late["final"] = tie(
            (*parts, late["attn"], branch_team, final)
        )
        late["out"] = outer_quarters(True, bits, attended, right)
        return parts

    def sums_on(parts):
        *parts, late["attn_far"], late["out"], total, own, near, relayed = tie(
            (*parts, late["attn_far"], late["out"], late["final"], gu_own, gu_near, gu_relay)
        )
        late["total"] = (middle + layout.scatter_add(total)).astype(BF16)
        late["attn_relay"] = layout.relay_sum(late["attn"][0], late["attn_far"], "grad_attn")
        late["out_far"] = swap(late["out"][3], layout.low, "grad_out_far")
        late["gate_up"] = sum_parts(BF16, (parts[0],), *zip(own, near, relayed))
        return parts

    grad_normed_attn = layout.scatter_rows(
        lambda core: dot(part(grad_qkv, core), w_attn_own, NT), (attn_terms, out_terms, sums_on)
    )
    attn_parts, out_parts = late["attn"], late["out"]
    grad_normed_attn, out_far, attn_sent, gu_sums = tie(
        (grad_normed_attn, late["out_far"], attn_parts[3], late["gate_up"])
    )
    grad_normed_attn, grad_down = tie((grad_normed_attn, grad_down))
    attn_relay = late["attn_relay"]
    attn_near = swap(attn_sent, layout.low, "grad_attn_near")
    out_relay = layout.relay_sum(out_parts[2], out_far, "grad_out")
    out_near = swap(out_parts[1], layout.low, "grad_out_near")
    grad_input = grad_middle + norm_back(grad_normed_attn, x_wide, gain_attn)
    grad_rows, attn_relay = tie((grad_input.astype(BF16), attn_relay))
    home = layout.from_team(jnp.concatenate([late["total"], grad_rows], axis=1), "rows_home")
    block_out, grad_input = home[..., :width], home[..., width:].astype(F32)

    by_member = lambda a: a.reshape(members, weight_rows, -1)
    dealt = layout.exchange(by_member(jnp.concatenate(gu_sums)))
    (grad_attn,) = sum_parts(BF16, (grad_rows, dealt), (attn_parts[2], attn_near, attn_relay))
    grad_attn = layout.rows_in(layout.exchange(by_member(grad_attn))).astype(F32)
    (grad_out,) = sum_parts(BF16, (grad_rows,), (out_parts[0], out_near, out_relay))
    grad_out = layout.cross(grad_out).astype(F32)
    grad_gate, grad_up = collect(places, dealt)

    def sum_kv(array):
        return array.reshape((KEY_VALUE_HEADS, -1) + array.shape[1:]).sum(1)

    def lay(array):
        return jnp.swapaxes(array, 0, 1).reshape(array.shape[1], -1)

    grad_query = lay(grad_attn[:, :, :query_width])
    grad_kv = sum_kv(grad_attn[:, :, query_width + padding :])
    grad_key = lay(grad_kv[:, :, :HEAD_WIDTH])
    grad_value = lay(grad_kv[:, :, HEAD_WIDTH:])

    def gain_gradient(gain, *terms):
        total = sum(jnp.sum(w.astype(F32) * grad, axis=1) for w, grad in terms)
        return total / gain.astype(F32)

    grad_norm_attn = gain_gradient(
        norm_attn, (w_query, grad_query), (key_weight, grad_key), (value_weight, grad_value)
    )
    grad_norm_mlp = gain_gradient(norm_mlp, (w_gate, grad_gate), (w_up, grad_up))

    return (
        block_out,
        grad_input,
        grad_norm_attn,
        grad_query,
        grad_key,
        grad_value,
        grad_out,
        grad_norm_mlp,
        grad_gate,
        grad_up,
        grad_down,
    )


def solution(mesh):
    layout = Layout(mesh)
    tokens = P("core", layout.ctx, None)
    rows = P(layout.all, None)
    line = P(layout.all)
    in_specs = (
        tokens, P(), P("core", None), line, rows, rows, rows, rows, line, rows, rows, rows, tokens,
    )
    out_specs = (tokens, tokens, line, rows, rows, rows, rows, line, rows, rows, rows)
    return jax.shard_map(
        functools.partial(shards, layout),
        mesh=layout.mesh,
        in_specs=in_specs,
        out_specs=out_specs,
        check_vma=False,
    )
```

```python
import functools
import math

import jax
import jax.numpy as jnp
from jax import lax
from jax.experimental import pallas as pl
from jax.experimental.pallas import tpu as pltpu
from jax.sharding import Mesh, PartitionSpec as P

QUERY_HEADS = 32
KEY_VALUE_HEADS = 4
HEAD_WIDTH = 64
GROUP = QUERY_HEADS // KEY_VALUE_HEADS
EPSILON = 1e-05
SCALE = 1.0 / math.sqrt(HEAD_WIDTH)
SWAP = ((0, 1), (1, 0))
CROSS = ((1, 2), (2, 1))
BF16 = jnp.bfloat16
F32 = jnp.float32
VMEM = 22 * 1024 * 1024
COST = pl.CostEstimate(flops=1, bytes_accessed=1, transcendentals=0)

NT = (((1,), (1,)), ((), ()))
TN = (((0,), (0,)), ((), ()))
NN = (((1,), (0,)), ((), ()))


def dot(left, right, dims=NN):
    return lax.dot_general(left, right, dims, preferred_element_type=F32)


def pick(array, index, axis=0):
    return lax.dynamic_index_in_dim(array, index, axis, keepdims=False)


def bit(axis):
    return lax.axis_index(axis)


def swap(array, axis, name="swap"):
    with jax.named_scope(name):
        return lax.ppermute(array, axis, SWAP)


def pair(axis, own, got, at=0):
    first = bit(axis) == 0
    return jnp.stack([jnp.where(first, own, got), jnp.where(first, got, own)], at)


def half_swap(array):
    width = array.shape[-1]
    lane = lax.broadcasted_iota(jnp.int32, array.shape, array.ndim - 1)
    ahead = pltpu.roll(array, width - HEAD_WIDTH // 2, array.ndim - 1)
    behind = pltpu.roll(array, HEAD_WIDTH // 2, array.ndim - 1)
    return jnp.where(lane % HEAD_WIDTH < HEAD_WIDTH // 2, ahead, behind)


def widen(table, width):
    return jnp.concatenate([table] * (width // table.shape[-1]), axis=-1)


def place_of(bits_ref, which):
    high = 1 - bits_ref[0] if which & 1 else bits_ref[0]
    low = 1 - bits_ref[1] if which & 2 else bits_ref[1]
    return high, low


def deal_attn_kernel(queries, kv_of, order, bits_ref, own, far, near, corner, out_ref, scratch):
    rows = own.shape[0]
    columns = out_ref.shape[-1]
    keys = own.shape[1] - 128 - 2 * KEY_VALUE_HEADS * HEAD_WIDTH
    values = keys + KEY_VALUE_HEADS * HEAD_WIDTH
    for which, ref in enumerate((own, far, near, corner)):
        high, low = place_of(bits_ref, which)
        scratch[2 * high + low] = ref[...]
    gains = [scratch[at, :, own.shape[1] - 128 :].astype(F32).T[:16] for at in range(4)]
    gains = jnp.concatenate(gains + [jnp.zeros((16, columns - 4 * rows), F32)], axis=1).astype(BF16)
    for slot, (member, kv) in enumerate(zip(order, kv_of)):
        for at in range(4):
            head = lambda start: scratch[at, :, start + kv * HEAD_WIDTH : start + (kv + 1) * HEAD_WIDTH]
            out_ref[slot, at * rows : (at + 1) * rows, :queries] = scratch[
                at, :, member * queries : (member + 1) * queries
            ]
            if queries < columns - 128:
                out_ref[slot, at * rows : (at + 1) * rows, queries : columns - 128] = jnp.zeros(
                    (rows, columns - 128 - queries), BF16
                )
            both = jnp.concatenate([head(keys), head(values)], axis=1)
            out_ref[slot, at * rows : (at + 1) * rows, columns - 128 :] = both
        out_ref[slot, 4 * rows :] = gains


def deal_attn(bits, order, kv_of, queries, padded, parts):
    rows, width = parts[0].shape
    columns = padded + 128
    shape = (len(order), 4 * rows + 16, columns)
    return pl.pallas_call(
        functools.partial(deal_attn_kernel, queries, kv_of, order),
        in_specs=[pl.BlockSpec(memory_space=pltpu.SMEM)]
        + [pl.BlockSpec(memory_space=pltpu.VMEM)] * 4,
        out_shape=jax.ShapeDtypeStruct(shape, BF16),
        scratch_shapes=[pltpu.VMEM((4, rows, width), BF16)],
        compiler_params=pltpu.CompilerParams(vmem_limit_bytes=VMEM),
        cost_estimate=COST,
        name="deal_attn",
    )(bits, *parts)


def project_kernel(
    x_ref, dealt_ref, cos_ref, sin_ref,
    normed_ref, q_ref, k_ref, v_ref, kt_ref, vt_ref, gains_ref, w_ref,
):
    width = q_ref.shape[-1]
    places, rows = w_ref.shape[1], w_ref.shape[4]

    @pl.when(pl.program_id(0) == 0)
    def _():
        gains = []
        for high in (0, 1):
            for place in range(places):
                for low in (0, 1):
                    for core in (0, 1):
                        at = slice((2 * high + low) * rows, (2 * high + low + 1) * rows)
                        w_ref[high, place, low, core] = dealt_ref[2 * place + core, at, :]
                        both = dealt_ref[2 * place + core, 4 * rows :, at]
                        gains.append(both.astype(F32)[:8])
        gains_ref[...] = jnp.concatenate(gains, axis=1)

    x = x_ref[...].astype(F32)
    r = lax.rsqrt(jnp.mean(x * x, axis=-1, keepdims=True) + EPSILON)
    normed = (x * r * gains_ref[:1, :]).astype(BF16)
    normed_ref[...] = normed
    w = w_ref[...].reshape(x_ref.shape[-1], w_ref.shape[-1])
    y = dot(normed, w)
    q = y[:, :width]
    both = y[:, width:]
    lane = lax.broadcasted_iota(jnp.int32, both.shape, 1)
    other = pltpu.roll(both, HEAD_WIDTH, 1)
    k = jnp.where(lane < HEAD_WIDTH, both, other)
    v = jnp.where(lane < HEAD_WIDTH, other, both)
    turn = lambda a: a * widen(cos_ref[...], a.shape[-1]) + half_swap(a) * widen(sin_ref[...], a.shape[-1])
    q_ref[...] = turn(q).astype(BF16)
    k = widen(turn(k), width)
    v = widen(v, width)
    k_ref[...] = k.astype(BF16)
    v_ref[...] = v.astype(BF16)
    kt_ref[...] = k.T.astype(BF16)
    vt_ref[...] = v.T.astype(BF16)


def project(places, x, dealt, cos, sin):
    rows, width = x.shape
    columns = dealt.shape[2]
    out = columns - 128
    block = 256
    row = lambda n: pl.BlockSpec((block, n), lambda i: (i, 0))
    across = pl.BlockSpec((out, block), lambda i: (0, i))
    shape = jax.ShapeDtypeStruct
    whole = (2, places, 2, 2, (dealt.shape[1] - 16) // 4, columns)
    return pl.pallas_call(
        project_kernel,
        grid=(rows // block,),
        in_specs=[row(width), pl.BlockSpec(dealt.shape, lambda i: (0, 0, 0)), row(128), row(128)],
        out_specs=[row(width), row(out), row(out), row(out), across, across]
        + [pl.BlockSpec((8, width), lambda i: (0, 0))]
        + [pl.BlockSpec(whole, lambda i: (0, 0, 0, 0, 0, 0))],
        out_shape=[shape((rows, n), BF16) for n in (width, out, out, out)]
        + [shape((out, rows), BF16)] * 2
        + [shape((8, width), F32), shape(whole, BF16)],
        compiler_params=pltpu.CompilerParams(vmem_limit_bytes=VMEM),
        cost_estimate=COST,
        name="project",
    )(x, dealt, cos, sin)


def visible_to(marks_all, marks):
    marks = marks.T
    return (marks_all[:, :1] <= marks[:1, :]) & (marks_all[:, 1:2] == marks[1:2, :])


def forward_kernel(heads, q_ref, k_ref, vt_ref, marks_ref, marks_all_ref, out_ref, lse_ref):
    q = q_ref[...]
    visible = visible_to(marks_all_ref[...], marks_ref[...])
    lane = lax.broadcasted_iota(jnp.int32, q.shape, 1) // HEAD_WIDTH
    wide = (q.shape[1], q.shape[0])
    row = lax.broadcasted_iota(jnp.int32, wide, 0) // HEAD_WIDTH
    total = jnp.zeros(wide, F32)
    lse_ref[...] = jnp.zeros_like(lse_ref)
    for head in range(heads):
        own = jnp.where(lane == head, q, jnp.zeros_like(q))
        scores = jnp.where(visible, dot(k_ref[...], own, NT) * SCALE, -1e30)
        top = jnp.max(scores, axis=0, keepdims=True)
        powers = jnp.exp(scores - top)
        mass = jnp.sum(powers, axis=0, keepdims=True)
        lse_ref[head : head + 1, :] = top + jnp.log(mass)
        chances = (powers * (1.0 / mass)).astype(BF16)
        total = jnp.where(row == head, dot(vt_ref[...], chances), total)
    out_ref[...] = total.T.astype(BF16)


def query_block(rows):
    return 256 if rows <= 1024 else 128


def attend_forward(heads, q, k, vt, marks):
    rows, width = q.shape
    block = query_block(rows)
    row = pl.BlockSpec((block, width), lambda i: (i, 0))
    mark = pl.BlockSpec((block, 128), lambda i: (i, 0))
    whole = lambda a: pl.BlockSpec(a.shape, lambda i: (0, 0))
    return pl.pallas_call(
        functools.partial(forward_kernel, heads),
        grid=(rows // block,),
        in_specs=[row, whole(k), whole(vt), mark, whole(marks)],
        out_specs=[row, pl.BlockSpec((8, block), lambda i: (0, i))],
        out_shape=[
            jax.ShapeDtypeStruct((rows, width), BF16),
            jax.ShapeDtypeStruct((8, rows), F32),
        ],
        compiler_params=pltpu.CompilerParams(vmem_limit_bytes=VMEM),
        cost_estimate=COST,
        name="attend_forward",
    )(q, k, vt, marks, marks)


def backward_kernel(
    heads, q_ref, g_ref, k_ref, v_ref, kt_ref, marks_ref, marks_all_ref, lse_ref,
    cos_ref, sin_ref, cos_all_ref, sin_all_ref, gq_ref, gkv_ref, gk_sum, gv_sum,
):
    step = pl.program_id(0)

    @pl.when(step == 0)
    def _():
        gk_sum[...] = jnp.zeros_like(gk_sum)
        gv_sum[...] = jnp.zeros_like(gv_sum)

    q = q_ref[...]
    g = g_ref[...]
    visible = visible_to(marks_all_ref[...], marks_ref[...])
    lane = lax.broadcasted_iota(jnp.int32, q.shape, 1) // HEAD_WIDTH
    wide = (q.shape[1], q.shape[0])
    row = lax.broadcasted_iota(jnp.int32, wide, 0) // HEAD_WIDTH
    total = jnp.zeros(wide, F32)
    for head in range(heads):
        own = jnp.where(lane == head, q, jnp.zeros_like(q))
        own_g = jnp.where(lane == head, g, jnp.zeros_like(g))
        scores = dot(k_ref[...], own, NT) * SCALE
        chances = jnp.where(visible, jnp.exp(scores - lse_ref[head : head + 1, :]), 0.0)
        grads = dot(v_ref[...], own_g, NT)
        inner = jnp.sum(chances * grads, axis=0, keepdims=True)
        grad_scores = (chances * (grads - inner)).astype(BF16)
        gv_sum[...] += dot(chances.astype(BF16), own_g)
        gk_sum[...] += dot(grad_scores, own)
        total = jnp.where(row == head, dot(kt_ref[...], grad_scores), total)
    gq = total.T * SCALE
    width = gq.shape[-1]
    gq = gq * widen(cos_ref[...], width) - half_swap(gq) * widen(sin_ref[...], width)
    gq_ref[...] = gq.astype(BF16)

    @pl.when(step == pl.num_programs(0) - 1)
    def _():
        def fold(array):
            parts = [array[:, at : at + 128] for at in range(0, array.shape[-1], 128)]
            both = functools.reduce(lambda a, b: a + b, parts)
            return both + pltpu.roll(both, HEAD_WIDTH, 1)

        gk = fold(gk_sum[...]) * SCALE
        gk = gk * cos_all_ref[...] - half_swap(gk) * sin_all_ref[...]
        gv = fold(gv_sum[...])
        lane = lax.broadcasted_iota(jnp.int32, gk.shape, 1)
        gkv_ref[...] = jnp.where(lane < HEAD_WIDTH, gk, gv).astype(BF16)


def attend_backward(heads, q, g, k, v, kt, marks, lse, cos, sin):
    rows, width = q.shape
    block = query_block(rows)
    row = lambda n: pl.BlockSpec((block, n), lambda i: (i, 0))
    across = lambda n: pl.BlockSpec((n, block), lambda i: (0, i))
    whole = lambda a: pl.BlockSpec(a.shape, lambda i: (0, 0))
    return pl.pallas_call(
        functools.partial(backward_kernel, heads),
        grid=(rows // block,),
        in_specs=[
            row(width), row(width), whole(k), whole(v), whole(kt), row(128), whole(marks),
            across(8), row(128), row(128), whole(cos), whole(sin),
        ],
        out_specs=[row(width), pl.BlockSpec((rows, 128), lambda i: (0, 0))],
        out_shape=[
            jax.ShapeDtypeStruct((rows, width), BF16),
            jax.ShapeDtypeStruct((rows, 128), BF16),
        ],
        scratch_shapes=[pltpu.VMEM((rows, width), F32), pltpu.VMEM((rows, width), F32)],
        compiler_params=pltpu.CompilerParams(vmem_limit_bytes=VMEM),
        cost_estimate=COST,
        name="attend_backward",
    )(q, g, k, v, kt, marks, marks, lse, cos, sin, cos, sin)


def feed_kernel(bits_ref, n_ref, g_ref, down_ref, *refs):
    parts = refs[:8]
    act_ref, back_ref, w_ref, sem = refs[8:]

    @pl.when(pl.program_id(0) == 0)
    def _():
        copies = []
        for at, part in enumerate(parts):
            which, chunk = at % 4, at // 4
            high, low = place_of(bits_ref, which)
            size = part.shape[0]
            places = pl.ds(chunk * size, size)
            copies.append(
                pltpu.make_async_copy(part, w_ref.at[high, places, low], sem.at[at])
            )
        for copy in copies:
            copy.start()
        for copy in copies:
            copy.wait()

    units = act_ref.shape[-1]
    both = dot(n_ref[...], w_ref[...].reshape(n_ref.shape[-1], 2 * units))
    gate, up = both[:, :units], both[:, units:]
    grad = dot(g_ref[...], down_ref[...], NT)
    s = jax.nn.sigmoid(gate)
    silu = gate * s
    act_ref[...] = (silu * up).astype(BF16)
    back = jnp.concatenate([grad * up * s * (1.0 + gate * (1.0 - s)), grad * silu], axis=1)
    back_ref[...] = back.astype(BF16)


def feed_forward(bits, n, g, down, parts):
    rows, width = n.shape
    places, piece, columns = parts[0].shape
    units = columns // 2
    block = 256
    row = lambda w: pl.BlockSpec((block, w), lambda i: (i, 0))
    whole = (2, 2 * places, 2, piece, columns)
    return pl.pallas_call(
        feed_kernel,
        grid=(rows // block,),
        in_specs=[
            pl.BlockSpec(memory_space=pltpu.SMEM),
            row(width),
            row(width),
            pl.BlockSpec(down.shape, lambda i: (0, 0)),
        ]
        + [pl.BlockSpec(memory_space=pl.ANY)] * 8,
        out_specs=[row(units), row(columns), pl.BlockSpec(whole, lambda i: (0, 0, 0, 0, 0))],
        out_shape=[
            jax.ShapeDtypeStruct((rows, units), BF16),
            jax.ShapeDtypeStruct((rows, columns), BF16),
            jax.ShapeDtypeStruct(whole, BF16),
        ],
        scratch_shapes=[pltpu.SemaphoreType.DMA((8,))],
        compiler_params=pltpu.CompilerParams(vmem_limit_bytes=VMEM),
        cost_estimate=COST,
        name="feed_forward",
    )(bits, n, g, down, *parts)


def rows_kernel(sides, chunks, bits_ref, left_ref, right_ref, *refs):
    outs, scratch = refs[:-1], refs[-1]
    step, chunk = pl.program_id(0), pl.program_id(1)
    low = bits_ref[1]
    scratch[...] = dot(left_ref[...], right_ref[...], TN).astype(BF16)
    for side in range(len(sides)):
        for part in range(chunks):

            @pl.when((step == side) & (chunk == part))
            def _():
                for beside in (0, 1):
                    out = outs[(side * 2 + beside) * chunks + part]
                    rows = out.shape[1]
                    column = 1 - low if beside else low
                    for place in range(out.shape[0]):
                        start = pl.multiple_of((2 * place + column) * rows, rows)
                        out[place] = scratch[pl.ds(start, rows), :]


def outer_rows(sides, chunks, places, bits, left, right):
    rows, width = left.shape
    columns = right.shape[1]
    piece = width // (4 * places)
    block = width // (2 * chunks)
    shape = (places // chunks, piece, columns)
    count = len(sides) * 2 * chunks
    first = sides[0]
    outs = pl.pallas_call(
        functools.partial(rows_kernel, sides, chunks),
        grid_spec=pltpu.PrefetchScalarGridSpec(
            num_scalar_prefetch=1,
            grid=(len(sides), chunks),
            in_specs=[
                pl.BlockSpec(
                    (rows, block),
                    lambda i, j, bits: (0, jnp.bitwise_xor(bits[0], jnp.bitwise_xor(i, first)) * chunks + j),
                ),
                pl.BlockSpec(right.shape, lambda i, j, bits: (0, 0)),
            ],
            out_specs=[pl.BlockSpec(shape, lambda i, j, bits: (0, 0, 0))] * count,
            scratch_shapes=[pltpu.VMEM((block, columns), BF16)],
        ),
        out_shape=[jax.ShapeDtypeStruct(shape, BF16)] * count,
        compiler_params=pltpu.CompilerParams(vmem_limit_bytes=VMEM),
        cost_estimate=COST,
        name="outer_rows",
    )(bits, left, right)
    return [list(outs[at : at + chunks]) for at in range(0, count, chunks)]


def quarters_kernel(flip, bits_ref, left_ref, right_ref, own, near, theirs, far, scratch):
    scratch[...] = dot(left_ref[...], right_ref[...], TN).astype(BF16)
    rows = own.shape[0]
    for ref, there, beside in ((own, 0, 0), (near, 0, 1), (theirs, 1, 0), (far, 1, 1)):
        high = 1 - bits_ref[0] if there else bits_ref[0]
        low = 1 - bits_ref[1] if beside else bits_ref[1]
        at = 2 * low + high if flip else 2 * high + low
        ref[...] = scratch[pl.ds(pl.multiple_of(at * rows, rows), rows), :]


def outer_quarters(flip, bits, left, right):
    rows, width = left.shape
    columns = right.shape[1]
    block = min(columns, 512)
    piece = width // 4
    if piece % 16:
        product = dot(left, right, TN).astype(BF16).reshape(2, 2, piece, columns)
        high, low = (bits[1], bits[0]) if flip else (bits[0], bits[1])
        sides = ((0, 0), (1, 0), (0, 1), (1, 1)) if flip else ((0, 0), (0, 1), (1, 0), (1, 1))
        return [pick(pick(product, high ^ a), low ^ b) for a, b in sides]
    return pl.pallas_call(
        functools.partial(quarters_kernel, flip),
        grid_spec=pltpu.PrefetchScalarGridSpec(
            num_scalar_prefetch=1,
            grid=(columns // block,),
            in_specs=[
                pl.BlockSpec(left.shape, lambda i, bits: (0, 0)),
                pl.BlockSpec((rows, block), lambda i, bits: (0, i)),
            ],
            out_specs=[pl.BlockSpec((piece, block), lambda i, bits: (0, i))] * 4,
            scratch_shapes=[pltpu.VMEM((width, block), BF16)],
        ),
        out_shape=[jax.ShapeDtypeStruct((piece, columns), BF16)] * 4,
        compiler_params=pltpu.CompilerParams(vmem_limit_bytes=VMEM),
        cost_estimate=COST,
        name="outer_quarters",
    )(bits, left, right)


def deal_kernel(places, gate_ref, up_ref, out_ref):
    rows, columns = gate_ref.shape
    piece = columns // (8 * places)
    for place in range(places):
        for core in (0, 1):
            starts = [
                (((high * places + place) * 2 + low) * 2 + core) * piece
                for high in (0, 1)
                for low in (0, 1)
            ]
            out_ref[2 * place + core] = jnp.concatenate(
                [ref[:, start : start + piece] for ref in (gate_ref, up_ref) for start in starts],
                axis=1,
            )


def deal(places, gate, up):
    rows, columns = gate.shape
    return pl.pallas_call(
        functools.partial(deal_kernel, places),
        out_shape=jax.ShapeDtypeStruct((2 * places, rows, columns // places), BF16),
        compiler_params=pltpu.CompilerParams(vmem_limit_bytes=VMEM),
        cost_estimate=COST,
        name="deal",
    )(gate, up)


def collect_kernel(places, in_ref, gate_ref, up_ref):
    rows, columns = gate_ref.shape
    piece = columns // (8 * places)
    for which, ref in enumerate((gate_ref, up_ref)):
        pieces = []
        for high in (0, 1):
            for place in range(places):
                for low in (0, 1):
                    for core in (0, 1):
                        start = (4 * which + 2 * high + low) * piece
                        got = in_ref[2 * place + core][:, start : start + piece]
                        pieces.append(got.astype(F32))
        ref[...] = jnp.concatenate(pieces, axis=1)


def collect(places, array):
    _, rows, columns = array.shape
    shape = jax.ShapeDtypeStruct((rows, places * columns), F32)
    return pl.pallas_call(
        functools.partial(collect_kernel, places),
        out_shape=[shape, shape],
        compiler_params=pltpu.CompilerParams(vmem_limit_bytes=VMEM),
        cost_estimate=COST,
        name="collect",
    )(array)


def sum_kernel(count, *refs):
    outs = refs[-count:]
    for at in range(count):
        own, near, relayed = refs[3 * at : 3 * at + 3]
        total = own[...].astype(F32) + near[...].astype(F32) + relayed[...].astype(F32)
        outs[at][...] = total.astype(outs[at].dtype)


def sum_parts(dtype, after, *groups):
    vmem = pl.BlockSpec(memory_space=pltpu.VMEM)
    return pl.pallas_call(
        functools.partial(sum_kernel, len(groups)),
        in_specs=[vmem] * (3 * len(groups)) + [pl.BlockSpec(memory_space=pl.ANY)] * len(after),
        out_shape=[jax.ShapeDtypeStruct(group[0].shape, dtype) for group in groups],
        compiler_params=pltpu.CompilerParams(vmem_limit_bytes=VMEM),
        cost_estimate=COST,
        name="sum_parts",
    )(*[part for group in groups for part in group], *after)


def row_tables(positions, docs):
    inverse = 10000.0 ** (-jnp.arange(0, HEAD_WIDTH, 2).astype(F32) / HEAD_WIDTH)
    angles = positions.astype(F32)[:, None] * inverse[None, :]
    cos, sin = jnp.cos(angles), jnp.sin(angles)
    marks = jnp.stack([positions, docs], axis=1).astype(F32)
    marks = jnp.pad(marks, ((0, 0), (0, 126)))
    return jnp.concatenate([cos] * 4, 1), jnp.concatenate([-sin, sin] * 2, 1), marks


def norm_back(upstream, values, gain):
    scaling = lax.rsqrt(jnp.mean(values * values, axis=-1, keepdims=True) + EPSILON)
    scaled_grad = upstream * gain
    return scaling * scaled_grad - values * (scaling * scaling * scaling) * jnp.mean(
        scaled_grad * values, axis=-1, keepdims=True
    )


class Layout:
    def __init__(self, mesh):
        bits = mesh.shape["ctx"].bit_length() - 1
        self.ctx = tuple(f"p{i}" for i in range(bits))
        self.mesh = Mesh(
            mesh.devices.reshape((2,) * bits + (mesh.shape["fsdp"],)), self.ctx + ("core",)
        )
        self.high, self.low = self.ctx[0], self.ctx[-1]
        self.mid = self.ctx[1:-1]
        self.places = 2 ** len(self.mid)
        self.members = 2 * self.places
        self.all = self.ctx + ("core",)
        self.turn = [
            [(4 * h + 2 * l + c, 4 * c + 2 * (l ^ other) + h) for h in (0, 1) for l in (0, 1) for c in (0, 1)]
            for other in (0, 1)
        ]

    def cross(self, array):
        got = lax.ppermute(array, (self.high, "core"), CROSS)
        return jnp.where(bit(self.high) == bit("core"), array, got)

    def turned(self, array, other, name):
        with jax.named_scope(name):
            return lax.ppermute(array, (self.high, self.low, "core"), self.turn[other])

    def to_team(self, array, name):
        low = bit(self.low)
        return self.turned(pick(array, low), 0, name), self.turned(pick(array, 1 - low), 1, name)

    def in_order(self, blocks):
        both = pair(self.low, *blocks)
        return both.reshape(-1, both.shape[-1])

    def from_team(self, array, name):
        low = bit(self.low)
        both = array.reshape(2, -1, array.shape[-1])
        return pair(
            self.low,
            self.turned(pick(both, low), 0, name),
            self.turned(pick(both, 1 - low), 1, name),
        )

    def team_gather(self, array):
        return lax.all_gather(array, ("core",) + self.mid, axis=0, tiled=True)


    def scatter_cores(self, rows_of, then=None):
        core = bit("core")
        sent = rows_of(1 - core).astype(BF16)
        got = swap(sent, "core", "sum_cores")
        if then is not None:
            then(sent)
        mine = rows_of(core) + got.astype(F32)
        width = mine.shape[1]
        mine = mine.astype(BF16).reshape((2,) * len(self.mid) + (-1, width))
        return [mine[..., : width // 2], mine[..., width // 2 :]]

    def scatter_send(self, parts, count):
        pending = []
        for part, order in zip(parts, (list(self.mid), list(self.mid[::-1]))):
            left = [axis for axis in self.mid if axis not in order[:count]]
            at = left.index(order[count])
            there = bit(order[count])
            pending.append((pick(part, there, at), swap(pick(part, 1 - there, at), order[count], f"sum_places_{count}")))
        return pending

    def scatter_add(self, pending):
        last = pending[0][0].ndim == 2
        parts = [own.astype(F32) + got.astype(F32) for own, got in pending]
        return jnp.concatenate(parts, 1) if last else [part.astype(BF16) for part in parts]

    def scatter_rows(self, rows_of, then=()):
        then = list(then) + [lambda parts: parts] * (1 + len(self.mid) - len(then))
        parts = self.scatter_cores(rows_of, then[0])
        for count in range(len(self.mid)):
            parts = self.scatter_add(self.scatter_send(then[1 + count](parts), count))
        return parts

    def exchange(self, array):
        return lax.all_to_all(array, self.mid + ("core",), 0, 0, tiled=True)

    def rows_out(self, array):
        shape = array.shape
        return jnp.swapaxes(array.reshape((2, self.places) + shape[1:]), 0, 1).reshape(shape)

    def rows_in(self, array):
        shape = array.shape
        return jnp.swapaxes(array.reshape((self.places, 2) + shape[1:]), 0, 1).reshape(shape)


    def start_four(self, array, name):
        return swap(array, self.high, name + "_far"), swap(array, self.low, name + "_near")

    def corner_four(self, far, name):
        return swap(far, self.low, name + "_corner")

    def join_four(self, first, second, own, far, near, corner):
        return pair(first, pair(second, own, near), pair(second, far, corner))

    def relay_sum(self, theirs, got_far, name):
        relay = theirs.astype(F32) + got_far.astype(F32)
        return swap(relay.astype(BF16), self.high, name + "_relay")


def shards(
    layout,
    hidden_in,
    positions,
    doc_ids,
    norm_attn,
    w_query,
    key_weight,
    value_weight,
    w_out,
    norm_mlp,
    w_gate,
    w_up,
    w_down,
    cotangent,
):
    members, places = layout.members, layout.places
    width = hidden_in.shape[-1]
    weight_rows = w_query.shape[0]
    heads = QUERY_HEADS // members
    padded = max(heads, 2)
    query_width = heads * HEAD_WIDTH
    padding = (padded - heads) * HEAD_WIDTH
    tie = lax.optimization_barrier
    place = sum(bit(axis) * 2**at for at, axis in enumerate(layout.mid[::-1]))
    bits = jnp.stack([bit(layout.high), bit(layout.low), 2 * place + bit("core")])
    bits = bits.astype(jnp.int32)
    order = [core * places + place for place in range(places) for core in (0, 1)]
    kv_of = [member * heads // GROUP for member in order]


    blocks = layout.to_team(hidden_in, "hidden")
    docs = layout.cross(pick(doc_ids, bit(layout.low)))
    gains = jnp.stack([norm_attn, norm_mlp], axis=1)
    gains = jnp.pad(gains, ((0, 0), (0, 126)))
    raw = jnp.concatenate([w_query, key_weight, value_weight, gains], axis=1)
    raw_far, raw_near = layout.start_four(raw, "raw")
    x = layout.in_order(blocks)
    x_team = layout.team_gather(x)
    cos, sin, marks = row_tables(positions, docs)
    dealt = deal(places, w_gate, w_up)
    raw_far, raw_near, w_out, cotangent, cos, sin, marks, dealt = tie(
        (raw_far, raw_near, w_out, cotangent, cos, sin, marks, dealt)
    )
    raw_corner = layout.corner_four(raw_far, "raw")
    out_part = layout.cross(w_out)
    g_blocks = layout.to_team(cotangent, "cotangent")
    dealt_attn = deal_attn(
        bits, order, kv_of, query_width, query_width + padding, (raw, raw_far, raw_near, raw_corner)
    )
    dealt_attn, out_part, w_down, *g_blocks = tie((dealt_attn, out_part, w_down, *g_blocks))
    dealt_attn = layout.exchange(dealt_attn)
    down_own = lax.all_gather(w_down, (layout.high, layout.low), axis=0, tiled=True)
    out_far, out_near = layout.start_four(out_part, "out")
    g_rows = layout.in_order(g_blocks)
    g = layout.team_gather(g_rows)
    dealt_attn, out_far, out_near, dealt = tie((dealt_attn, out_far, out_near, dealt))
    dealt = layout.exchange(dealt)
    out_corner = layout.corner_four(out_far, "out")

    normed_attn, q, k, v, kt, vt, gains, w_attn = project(places, x_team, dealt_attn, cos, sin)
    gain_attn, gain_mlp = gains[:1], gains[1:2]
    attended, lse = attend_forward(heads, q, k, vt, marks)
    attended, out_corner, dealt = tie((attended, out_corner, dealt))
    dealt = dealt.reshape(places, 2 * weight_rows, -1)
    chunk = lambda a, at: a[at * places // 2 : (at + 1) * places // 2]
    gu_parts = [chunk(dealt, 0), chunk(dealt, 1)]
    gu_far, gu_near, gu_corner = [None] * 2, [None] * 2, [None] * 2
    gu_far[0], gu_near[0] = layout.start_four(gu_parts[0], "gate_up_0")
    out_own = layout.join_four(layout.low, layout.high, out_part, out_near, out_far, out_corner)
    out_own = out_own.reshape(query_width, width)
    attended = attended[:, :query_width]

    half = x_team.shape[0] // 2
    part = lambda a, core: lax.dynamic_slice_in_dim(a, core * half, half, 0)
    same = lambda parts: parts
    late = {}

    def weights_on(parts):
        *parts, gu_far[0], gu_near[0], gu_parts[1] = tie(
            (*parts, gu_far[0], gu_near[0], gu_parts[1])
        )
        gu_corner[0] = layout.corner_four(gu_far[0], "gate_up_0")
        gu_far[1], gu_near[1] = layout.start_four(gu_parts[1], "gate_up_1")
        return parts

    branch = layout.scatter_rows(lambda core: dot(part(attended, core), out_own))
    (branch,) = weights_on((branch,))
    x_wide = x.astype(F32)
    middle = x_wide + branch
    scale_mlp = lax.rsqrt(jnp.mean(middle * middle, axis=-1, keepdims=True) + EPSILON)
    normed_mlp = layout.team_gather((middle * scale_mlp * gain_mlp).astype(BF16))
    gu_corner[1] = layout.corner_four(gu_far[1], "gate_up_1")

    activated, grad_gu, w_gu = feed_forward(
        bits,
        normed_mlp,
        g,
        down_own,
        [
            parts[at]
            for at in range(2)
            for parts in (gu_parts, gu_far, gu_near, gu_corner)
        ],
    )
    w_gu = w_gu.reshape(width, -1)

    def gu_terms(parts):
        *parts, right = tie((*parts, grad_gu))
        late["theirs"], late["far"] = outer_rows((1,), 2, places, bits, normed_mlp, right)
        return parts

    def gu_others(parts):
        *parts, late["far"], late["theirs"], right = tie(
            (*parts, late["far"], late["theirs"], grad_gu)
        )
        late["far"][0] = swap(late["far"][0], layout.low, "grad_gate_up_far_0")
        late["own"], late["near"] = outer_rows((0,), 2, places, bits, normed_mlp, right)
        return parts

    grad_normed_mlp = layout.scatter_rows(
        lambda core: dot(part(grad_gu, core), w_gu, NT), (None, gu_terms, gu_others)
    )
    gu_theirs, gu_far, gu_own, gu_near = (late[key] for key in ("theirs", "far", "own", "near"))
    grad_normed_mlp, gu_own, gu_near, gu_far[0] = tie((grad_normed_mlp, gu_own, gu_near, gu_far[0]))
    grad_middle = g_rows.astype(F32) + norm_back(grad_normed_mlp, middle, gain_mlp)
    grad_branch = grad_middle.astype(BF16)
    branch_team = layout.team_gather(grad_branch)
    gu_far[0], act, grad_branch, sent = tie((gu_far[0], activated, grad_branch, gu_far[1]))
    gu_relay = [layout.relay_sum(gu_theirs[0], gu_far[0], "grad_gate_up_0")]
    gu_far[1] = swap(sent, layout.low, "grad_gate_up_far_1")
    grad_down = dot(act, g, TN).astype(BF16)
    act, grad_down = tie((act, grad_down))
    final = layout.scatter_cores(lambda core: dot(part(act, core), down_own))
    branch_team, grad_down, gu_far[1], gu_relay[0], gu_near, *final = tie(
        (branch_team, grad_down, gu_far[1], gu_relay[0], gu_near, *final)
    )
    gu_relay.append(layout.relay_sum(gu_theirs[1], gu_far[1], "grad_gate_up_1"))
    gu_near = [swap(near, layout.low, f"grad_gate_up_near_{at}") for at, near in enumerate(gu_near)]
    grad_down = lax.psum_scatter(
        grad_down, (layout.high, layout.low), scatter_dimension=0, tiled=True
    ).astype(F32)
    final = layout.scatter_send(final, 0)
    grad_attended = dot(branch_team, out_own, NT).astype(BF16)
    if padding:
        grad_attended = jnp.pad(grad_attended, ((0, 0), (0, padding)))

    gq, gkv = attend_backward(heads, q, grad_attended, k, v, kt, marks, lse, cos, sin)
    grad_qkv = jnp.concatenate([gq, gkv], axis=1)
    grad_qkv, final, gu_near, gu_relay[1] = tie((grad_qkv, final, gu_near, gu_relay[1]))
    for count in range(1, len(layout.mid)):
        final = layout.scatter_send(layout.scatter_add(final), count)

    w_attn_own = w_attn.reshape(width, -1)[:, : grad_qkv.shape[1]]

    def attn_terms(sent):
        _, right = tie((sent, grad_qkv))
        late["attn"] = [part for (part,) in outer_rows((1, 0), 1, places, bits, normed_attn, right)]
        late["attn_far"] = swap(late["attn"][1], layout.low, "grad_attn_far")

    def out_terms(parts):
        *parts, late["attn"], right, late["final"] = tie(
            (*parts, late["attn"], branch_team, final)
        )
        late["out"] = outer_quarters(True, bits, attended, right)
        return parts

    def sums_on(parts):
        *parts, late["attn_far"], late["out"], total, own, near, relayed = tie(
            (*parts, late["attn_far"], late["out"], late["final"], gu_own, gu_near, gu_relay)
        )
        late["total"] = (middle + layout.scatter_add(total)).astype(BF16)
        late["attn_relay"] = layout.relay_sum(late["attn"][0], late["attn_far"], "grad_attn")
        late["out_far"] = swap(late["out"][3], layout.low, "grad_out_far")
        late["gate_up"] = sum_parts(BF16, (parts[0],), *zip(own, near, relayed))
        return parts

    grad_normed_attn = layout.scatter_rows(
        lambda core: dot(part(grad_qkv, core), w_attn_own, NT), (attn_terms, out_terms, sums_on)
    )
    attn_parts, out_parts = late["attn"], late["out"]
    grad_normed_attn, out_far, attn_sent, gu_sums = tie(
        (grad_normed_attn, late["out_far"], attn_parts[3], late["gate_up"])
    )
    grad_normed_attn, grad_down = tie((grad_normed_attn, grad_down))
    attn_relay = late["attn_relay"]
    attn_near = swap(attn_sent, layout.low, "grad_attn_near")
    out_relay = layout.relay_sum(out_parts[2], out_far, "grad_out")
    out_near = swap(out_parts[1], layout.low, "grad_out_near")
    grad_input = grad_middle + norm_back(grad_normed_attn, x_wide, gain_attn)
    grad_rows = grad_input.astype(BF16)
    home = layout.from_team(jnp.concatenate([late["total"], grad_rows], axis=1), "rows_home")
    block_out, grad_input = home[..., :width], home[..., width:].astype(F32)

    by_member = lambda a: a.reshape(members, weight_rows, -1)
    dealt = layout.exchange(by_member(jnp.concatenate(gu_sums)))
    (grad_attn,) = sum_parts(BF16, (grad_rows, dealt), (attn_parts[2], attn_near, attn_relay))
    grad_attn = layout.rows_in(layout.exchange(by_member(grad_attn))).astype(F32)
    (grad_out,) = sum_parts(BF16, (grad_rows,), (out_parts[0], out_near, out_relay))
    grad_out = layout.cross(grad_out).astype(F32)
    grad_gate, grad_up = collect(places, dealt)

    def sum_kv(array):
        return array.reshape((KEY_VALUE_HEADS, -1) + array.shape[1:]).sum(1)

    def lay(array):
        return jnp.swapaxes(array, 0, 1).reshape(array.shape[1], -1)

    grad_query = lay(grad_attn[:, :, :query_width])
    grad_kv = sum_kv(grad_attn[:, :, query_width + padding :])
    grad_key = lay(grad_kv[:, :, :HEAD_WIDTH])
    grad_value = lay(grad_kv[:, :, HEAD_WIDTH:])

    def gain_gradient(gain, *terms):
        total = sum(jnp.sum(w.astype(F32) * grad, axis=1) for w, grad in terms)
        return total / gain.astype(F32)

    grad_norm_attn = gain_gradient(
        norm_attn, (w_query, grad_query), (key_weight, grad_key), (value_weight, grad_value)
    )
    grad_norm_mlp = gain_gradient(norm_mlp, (w_gate, grad_gate), (w_up, grad_up))

    return (
        block_out,
        grad_input,
        grad_norm_attn,
        grad_query,
        grad_key,
        grad_value,
        grad_out,
        grad_norm_mlp,
        grad_gate,
        grad_up,
        grad_down,
    )


def solution(mesh):
    layout = Layout(mesh)
    tokens = P("core", layout.ctx, None)
    rows = P(layout.all, None)
    line = P(layout.all)
    in_specs = (
        tokens, P(), P("core", None), line, rows, rows, rows, rows, line, rows, rows, rows, tokens,
    )
    out_specs = (tokens, tokens, line, rows, rows, rows, rows, line, rows, rows, rows)
    return jax.shard_map(
        functools.partial(shards, layout),
        mesh=layout.mesh,
        in_specs=in_specs,
        out_specs=out_specs,
        check_vma=False,
    )
```

```python
import functools
import math

import jax
import jax.numpy as jnp
from jax import lax
from jax.experimental import pallas as pl
from jax.experimental.pallas import tpu as pltpu
from jax.sharding import Mesh, PartitionSpec as P

QUERY_HEADS = 32
KEY_VALUE_HEADS = 4
HEAD_WIDTH = 64
GROUP = QUERY_HEADS // KEY_VALUE_HEADS
EPSILON = 1e-05
SCALE = 1.0 / math.sqrt(HEAD_WIDTH)
SWAP = ((0, 1), (1, 0))
CROSS = ((1, 2), (2, 1))
BF16 = jnp.bfloat16
F32 = jnp.float32
VMEM = 22 * 1024 * 1024
COST = pl.CostEstimate(flops=1, bytes_accessed=1, transcendentals=0)

NT = (((1,), (1,)), ((), ()))
TN = (((0,), (0,)), ((), ()))
NN = (((1,), (0,)), ((), ()))


def dot(left, right, dims=NN):
    return lax.dot_general(left, right, dims, preferred_element_type=F32)


def pick(array, index, axis=0):
    return lax.dynamic_index_in_dim(array, index, axis, keepdims=False)


def bit(axis):
    return lax.axis_index(axis)


def swap(array, axis, name="swap"):
    with jax.named_scope(name):
        return lax.ppermute(array, axis, SWAP)


def pair(axis, own, got, at=0):
    first = bit(axis) == 0
    return jnp.stack([jnp.where(first, own, got), jnp.where(first, got, own)], at)


def half_swap(array):
    width = array.shape[-1]
    lane = lax.broadcasted_iota(jnp.int32, array.shape, array.ndim - 1)
    ahead = pltpu.roll(array, width - HEAD_WIDTH // 2, array.ndim - 1)
    behind = pltpu.roll(array, HEAD_WIDTH // 2, array.ndim - 1)
    return jnp.where(lane % HEAD_WIDTH < HEAD_WIDTH // 2, ahead, behind)


def widen(table, width):
    return jnp.concatenate([table] * (width // table.shape[-1]), axis=-1)


def place_of(bits_ref, which):
    high = 1 - bits_ref[0] if which & 1 else bits_ref[0]
    low = 1 - bits_ref[1] if which & 2 else bits_ref[1]
    return high, low


def deal_attn_kernel(queries, kv_of, order, bits_ref, own, far, near, corner, out_ref, scratch):
    rows = own.shape[0]
    columns = out_ref.shape[-1]
    keys = own.shape[1] - 128 - 2 * KEY_VALUE_HEADS * HEAD_WIDTH
    values = keys + KEY_VALUE_HEADS * HEAD_WIDTH
    for which, ref in enumerate((own, far, near, corner)):
        high, low = place_of(bits_ref, which)
        scratch[2 * high + low] = ref[...]
    gains = [scratch[at, :, own.shape[1] - 128 :].astype(F32).T[:16] for at in range(4)]
    gains = jnp.concatenate(gains + [jnp.zeros((16, columns - 4 * rows), F32)], axis=1).astype(BF16)
    for slot, (member, kv) in enumerate(zip(order, kv_of)):
        for at in range(4):
            head = lambda start: scratch[at, :, start + kv * HEAD_WIDTH : start + (kv + 1) * HEAD_WIDTH]
            out_ref[slot, at * rows : (at + 1) * rows, :queries] = scratch[
                at, :, member * queries : (member + 1) * queries
            ]
            if queries < columns - 128:
                out_ref[slot, at * rows : (at + 1) * rows, queries : columns - 128] = jnp.zeros(
                    (rows, columns - 128 - queries), BF16
                )
            both = jnp.concatenate([head(keys), head(values)], axis=1)
            out_ref[slot, at * rows : (at + 1) * rows, columns - 128 :] = both
        out_ref[slot, 4 * rows :] = gains


def deal_attn(bits, order, kv_of, queries, padded, parts):
    rows, width = parts[0].shape
    columns = padded + 128
    shape = (len(order), 4 * rows + 16, columns)
    return pl.pallas_call(
        functools.partial(deal_attn_kernel, queries, kv_of, order),
        in_specs=[pl.BlockSpec(memory_space=pltpu.SMEM)]
        + [pl.BlockSpec(memory_space=pltpu.VMEM)] * 4,
        out_shape=jax.ShapeDtypeStruct(shape, BF16),
        scratch_shapes=[pltpu.VMEM((4, rows, width), BF16)],
        compiler_params=pltpu.CompilerParams(vmem_limit_bytes=VMEM),
        cost_estimate=COST,
        name="deal_attn",
    )(bits, *parts)


def project_kernel(
    x_ref, dealt_ref, cos_ref, sin_ref,
    normed_ref, q_ref, k_ref, v_ref, kt_ref, vt_ref, gains_ref, w_ref,
):
    width = q_ref.shape[-1]
    places, rows = w_ref.shape[1], w_ref.shape[4]

    @pl.when(pl.program_id(0) == 0)
    def _():
        gains = []
        for high in (0, 1):
            for place in range(places):
                for low in (0, 1):
                    for core in (0, 1):
                        at = slice((2 * high + low) * rows, (2 * high + low + 1) * rows)
                        w_ref[high, place, low, core] = dealt_ref[2 * place + core, at, :]
                        both = dealt_ref[2 * place + core, 4 * rows :, at]
                        gains.append(both.astype(F32)[:8])
        gains_ref[...] = jnp.concatenate(gains, axis=1)

    x = x_ref[...].astype(F32)
    r = lax.rsqrt(jnp.mean(x * x, axis=-1, keepdims=True) + EPSILON)
    normed = (x * r * gains_ref[:1, :]).astype(BF16)
    normed_ref[...] = normed
    w = w_ref[...].reshape(x_ref.shape[-1], w_ref.shape[-1])
    y = dot(normed, w)
    q = y[:, :width]
    both = y[:, width:]
    lane = lax.broadcasted_iota(jnp.int32, both.shape, 1)
    other = pltpu.roll(both, HEAD_WIDTH, 1)
    k = jnp.where(lane < HEAD_WIDTH, both, other)
    v = jnp.where(lane < HEAD_WIDTH, other, both)
    turn = lambda a: a * widen(cos_ref[...], a.shape[-1]) + half_swap(a) * widen(sin_ref[...], a.shape[-1])
    q_ref[...] = turn(q).astype(BF16)
    k = widen(turn(k), width)
    v = widen(v, width)
    k_ref[...] = k.astype(BF16)
    v_ref[...] = v.astype(BF16)
    kt_ref[...] = k.T.astype(BF16)
    vt_ref[...] = v.T.astype(BF16)


def project(places, x, dealt, cos, sin):
    rows, width = x.shape
    columns = dealt.shape[2]
    out = columns - 128
    block = 256
    row = lambda n: pl.BlockSpec((block, n), lambda i: (i, 0))
    across = pl.BlockSpec((out, block), lambda i: (0, i))
    shape = jax.ShapeDtypeStruct
    whole = (2, places, 2, 2, (dealt.shape[1] - 16) // 4, columns)
    return pl.pallas_call(
        project_kernel,
        grid=(rows // block,),
        in_specs=[row(width), pl.BlockSpec(dealt.shape, lambda i: (0, 0, 0)), row(128), row(128)],
        out_specs=[row(width), row(out), row(out), row(out), across, across]
        + [pl.BlockSpec((8, width), lambda i: (0, 0))]
        + [pl.BlockSpec(whole, lambda i: (0, 0, 0, 0, 0, 0))],
        out_shape=[shape((rows, n), BF16) for n in (width, out, out, out)]
        + [shape((out, rows), BF16)] * 2
        + [shape((8, width), F32), shape(whole, BF16)],
        compiler_params=pltpu.CompilerParams(vmem_limit_bytes=VMEM),
        cost_estimate=COST,
        name="project",
    )(x, dealt, cos, sin)


def visible_to(marks_all, marks):
    marks = marks.T
    return (marks_all[:, :1] <= marks[:1, :]) & (marks_all[:, 1:2] == marks[1:2, :])


def forward_kernel(heads, q_ref, k_ref, vt_ref, marks_ref, marks_all_ref, out_ref, lse_ref):
    q = q_ref[...]
    visible = visible_to(marks_all_ref[...], marks_ref[...])
    lane = lax.broadcasted_iota(jnp.int32, q.shape, 1) // HEAD_WIDTH
    wide = (q.shape[1], q.shape[0])
    row = lax.broadcasted_iota(jnp.int32, wide, 0) // HEAD_WIDTH
    total = jnp.zeros(wide, F32)
    lse_ref[...] = jnp.zeros_like(lse_ref)
    for head in range(heads):
        own = jnp.where(lane == head, q, jnp.zeros_like(q))
        scores = jnp.where(visible, dot(k_ref[...], own, NT) * SCALE, -1e30)
        top = jnp.max(scores, axis=0, keepdims=True)
        powers = jnp.exp(scores - top)
        mass = jnp.sum(powers, axis=0, keepdims=True)
        lse_ref[head : head + 1, :] = top + jnp.log(mass)
        chances = (powers * (1.0 / mass)).astype(BF16)
        total = jnp.where(row == head, dot(vt_ref[...], chances), total)
    out_ref[...] = total.T.astype(BF16)


def query_block(rows):
    return 256 if rows <= 1024 else 128


def attend_forward(heads, q, k, vt, marks):
    rows, width = q.shape
    block = query_block(rows)
    row = pl.BlockSpec((block, width), lambda i: (i, 0))
    mark = pl.BlockSpec((block, 128), lambda i: (i, 0))
    whole = lambda a: pl.BlockSpec(a.shape, lambda i: (0, 0))
    return pl.pallas_call(
        functools.partial(forward_kernel, heads),
        grid=(rows // block,),
        in_specs=[row, whole(k), whole(vt), mark, whole(marks)],
        out_specs=[row, pl.BlockSpec((8, block), lambda i: (0, i))],
        out_shape=[
            jax.ShapeDtypeStruct((rows, width), BF16),
            jax.ShapeDtypeStruct((8, rows), F32),
        ],
        compiler_params=pltpu.CompilerParams(vmem_limit_bytes=VMEM),
        cost_estimate=COST,
        name="attend_forward",
    )(q, k, vt, marks, marks)


def backward_kernel(
    heads, q_ref, g_ref, k_ref, v_ref, kt_ref, marks_ref, marks_all_ref, lse_ref,
    cos_ref, sin_ref, cos_all_ref, sin_all_ref, gq_ref, gkv_ref, gk_sum, gv_sum,
):
    step = pl.program_id(0)

    @pl.when(step == 0)
    def _():
        gk_sum[...] = jnp.zeros_like(gk_sum)
        gv_sum[...] = jnp.zeros_like(gv_sum)

    q = q_ref[...]
    g = g_ref[...]
    visible = visible_to(marks_all_ref[...], marks_ref[...])
    lane = lax.broadcasted_iota(jnp.int32, q.shape, 1) // HEAD_WIDTH
    wide = (q.shape[1], q.shape[0])
    row = lax.broadcasted_iota(jnp.int32, wide, 0) // HEAD_WIDTH
    total = jnp.zeros(wide, F32)
    for head in range(heads):
        own = jnp.where(lane == head, q, jnp.zeros_like(q))
        own_g = jnp.where(lane == head, g, jnp.zeros_like(g))
        scores = dot(k_ref[...], own, NT) * SCALE
        chances = jnp.where(visible, jnp.exp(scores - lse_ref[head : head + 1, :]), 0.0)
        grads = dot(v_ref[...], own_g, NT)
        inner = jnp.sum(chances * grads, axis=0, keepdims=True)
        grad_scores = (chances * (grads - inner)).astype(BF16)
        gv_sum[...] += dot(chances.astype(BF16), own_g)
        gk_sum[...] += dot(grad_scores, own)
        total = jnp.where(row == head, dot(kt_ref[...], grad_scores), total)
    gq = total.T * SCALE
    width = gq.shape[-1]
    gq = gq * widen(cos_ref[...], width) - half_swap(gq) * widen(sin_ref[...], width)
    gq_ref[...] = gq.astype(BF16)

    @pl.when(step == pl.num_programs(0) - 1)
    def _():
        def fold(array):
            parts = [array[:, at : at + 128] for at in range(0, array.shape[-1], 128)]
            both = functools.reduce(lambda a, b: a + b, parts)
            return both + pltpu.roll(both, HEAD_WIDTH, 1)

        gk = fold(gk_sum[...]) * SCALE
        gk = gk * cos_all_ref[...] - half_swap(gk) * sin_all_ref[...]
        gv = fold(gv_sum[...])
        lane = lax.broadcasted_iota(jnp.int32, gk.shape, 1)
        gkv_ref[...] = jnp.where(lane < HEAD_WIDTH, gk, gv).astype(BF16)


def attend_backward(heads, q, g, k, v, kt, marks, lse, cos, sin):
    rows, width = q.shape
    block = query_block(rows)
    row = lambda n: pl.BlockSpec((block, n), lambda i: (i, 0))
    across = lambda n: pl.BlockSpec((n, block), lambda i: (0, i))
    whole = lambda a: pl.BlockSpec(a.shape, lambda i: (0, 0))
    return pl.pallas_call(
        functools.partial(backward_kernel, heads),
        grid=(rows // block,),
        in_specs=[
            row(width), row(width), whole(k), whole(v), whole(kt), row(128), whole(marks),
            across(8), row(128), row(128), whole(cos), whole(sin),
        ],
        out_specs=[row(width), pl.BlockSpec((rows, 128), lambda i: (0, 0))],
        out_shape=[
            jax.ShapeDtypeStruct((rows, width), BF16),
            jax.ShapeDtypeStruct((rows, 128), BF16),
        ],
        scratch_shapes=[pltpu.VMEM((rows, width), F32), pltpu.VMEM((rows, width), F32)],
        compiler_params=pltpu.CompilerParams(vmem_limit_bytes=VMEM),
        cost_estimate=COST,
        name="attend_backward",
    )(q, g, k, v, kt, marks, marks, lse, cos, sin, cos, sin)


def feed_kernel(bits_ref, n_ref, g_ref, down_ref, *refs):
    parts = refs[:8]
    act_ref, back_ref, w_ref, sem = refs[8:]

    @pl.when(pl.program_id(0) == 0)
    def _():
        copies = []
        for at, part in enumerate(parts):
            which, chunk = at % 4, at // 4
            high, low = place_of(bits_ref, which)
            size = part.shape[0]
            places = pl.ds(chunk * size, size)
            copies.append(
                pltpu.make_async_copy(part, w_ref.at[high, places, low], sem.at[at])
            )
        for copy in copies:
            copy.start()
        for copy in copies:
            copy.wait()

    units = act_ref.shape[-1]
    both = dot(n_ref[...], w_ref[...].reshape(n_ref.shape[-1], 2 * units))
    gate, up = both[:, :units], both[:, units:]
    grad = dot(g_ref[...], down_ref[...], NT)
    s = jax.nn.sigmoid(gate)
    silu = gate * s
    act_ref[...] = (silu * up).astype(BF16)
    back = jnp.concatenate([grad * up * s * (1.0 + gate * (1.0 - s)), grad * silu], axis=1)
    back_ref[...] = back.astype(BF16)


def feed_forward(bits, n, g, down, parts):
    rows, width = n.shape
    places, piece, columns = parts[0].shape
    units = columns // 2
    block = 256
    row = lambda w: pl.BlockSpec((block, w), lambda i: (i, 0))
    whole = (2, 2 * places, 2, piece, columns)
    return pl.pallas_call(
        feed_kernel,
        grid=(rows // block,),
        in_specs=[
            pl.BlockSpec(memory_space=pltpu.SMEM),
            row(width),
            row(width),
            pl.BlockSpec(down.shape, lambda i: (0, 0)),
        ]
        + [pl.BlockSpec(memory_space=pl.ANY)] * 8,
        out_specs=[row(units), row(columns), pl.BlockSpec(whole, lambda i: (0, 0, 0, 0, 0))],
        out_shape=[
            jax.ShapeDtypeStruct((rows, units), BF16),
            jax.ShapeDtypeStruct((rows, columns), BF16),
            jax.ShapeDtypeStruct(whole, BF16),
        ],
        scratch_shapes=[pltpu.SemaphoreType.DMA((8,))],
        compiler_params=pltpu.CompilerParams(vmem_limit_bytes=VMEM),
        cost_estimate=COST,
        name="feed_forward",
    )(bits, n, g, down, *parts)


def rows_kernel(sides, chunks, bits_ref, left_ref, right_ref, *refs):
    outs, scratch = refs[:-1], refs[-1]
    step, chunk = pl.program_id(0), pl.program_id(1)
    low = bits_ref[1]
    scratch[...] = dot(left_ref[...], right_ref[...], TN).astype(BF16)
    for side in range(len(sides)):
        for part in range(chunks):

            @pl.when((step == side) & (chunk == part))
            def _():
                for beside in (0, 1):
                    out = outs[(side * 2 + beside) * chunks + part]
                    rows = out.shape[1]
                    column = 1 - low if beside else low
                    for place in range(out.shape[0]):
                        start = pl.multiple_of((2 * place + column) * rows, rows)
                        out[place] = scratch[pl.ds(start, rows), :]


def outer_rows(sides, chunks, places, bits, left, right):
    rows, width = left.shape
    columns = right.shape[1]
    piece = width // (4 * places)
    block = width // (2 * chunks)
    shape = (places // chunks, piece, columns)
    count = len(sides) * 2 * chunks
    first = sides[0]
    outs = pl.pallas_call(
        functools.partial(rows_kernel, sides, chunks),
        grid_spec=pltpu.PrefetchScalarGridSpec(
            num_scalar_prefetch=1,
            grid=(len(sides), chunks),
            in_specs=[
                pl.BlockSpec(
                    (rows, block),
                    lambda i, j, bits: (0, jnp.bitwise_xor(bits[0], jnp.bitwise_xor(i, first)) * chunks + j),
                ),
                pl.BlockSpec(right.shape, lambda i, j, bits: (0, 0)),
            ],
            out_specs=[pl.BlockSpec(shape, lambda i, j, bits: (0, 0, 0))] * count,
            scratch_shapes=[pltpu.VMEM((block, columns), BF16)],
        ),
        out_shape=[jax.ShapeDtypeStruct(shape, BF16)] * count,
        compiler_params=pltpu.CompilerParams(vmem_limit_bytes=VMEM),
        cost_estimate=COST,
        name="outer_rows",
    )(bits, left, right)
    return [list(outs[at : at + chunks]) for at in range(0, count, chunks)]


def quarters_kernel(flip, bits_ref, left_ref, right_ref, own, near, theirs, far, scratch):
    scratch[...] = dot(left_ref[...], right_ref[...], TN).astype(BF16)
    rows = own.shape[0]
    for ref, there, beside in ((own, 0, 0), (near, 0, 1), (theirs, 1, 0), (far, 1, 1)):
        high = 1 - bits_ref[0] if there else bits_ref[0]
        low = 1 - bits_ref[1] if beside else bits_ref[1]
        at = 2 * low + high if flip else 2 * high + low
        ref[...] = scratch[pl.ds(pl.multiple_of(at * rows, rows), rows), :]


def outer_quarters(flip, bits, left, right):
    rows, width = left.shape
    columns = right.shape[1]
    block = min(columns, 512)
    piece = width // 4
    if piece % 16:
        product = dot(left, right, TN).astype(BF16).reshape(2, 2, piece, columns)
        high, low = (bits[1], bits[0]) if flip else (bits[0], bits[1])
        sides = ((0, 0), (1, 0), (0, 1), (1, 1)) if flip else ((0, 0), (0, 1), (1, 0), (1, 1))
        return [pick(pick(product, high ^ a), low ^ b) for a, b in sides]
    return pl.pallas_call(
        functools.partial(quarters_kernel, flip),
        grid_spec=pltpu.PrefetchScalarGridSpec(
            num_scalar_prefetch=1,
            grid=(columns // block,),
            in_specs=[
                pl.BlockSpec(left.shape, lambda i, bits: (0, 0)),
                pl.BlockSpec((rows, block), lambda i, bits: (0, i)),
            ],
            out_specs=[pl.BlockSpec((piece, block), lambda i, bits: (0, i))] * 4,
            scratch_shapes=[pltpu.VMEM((width, block), BF16)],
        ),
        out_shape=[jax.ShapeDtypeStruct((piece, columns), BF16)] * 4,
        compiler_params=pltpu.CompilerParams(vmem_limit_bytes=VMEM),
        cost_estimate=COST,
        name="outer_quarters",
    )(bits, left, right)


def deal_kernel(places, gate_ref, up_ref, out_ref):
    rows, columns = gate_ref.shape
    piece = columns // (8 * places)
    for place in range(places):
        for core in (0, 1):
            starts = [
                (((high * places + place) * 2 + low) * 2 + core) * piece
                for high in (0, 1)
                for low in (0, 1)
            ]
            out_ref[2 * place + core] = jnp.concatenate(
                [ref[:, start : start + piece] for ref in (gate_ref, up_ref) for start in starts],
                axis=1,
            )


def deal(places, gate, up):
    rows, columns = gate.shape
    return pl.pallas_call(
        functools.partial(deal_kernel, places),
        out_shape=jax.ShapeDtypeStruct((2 * places, rows, columns // places), BF16),
        compiler_params=pltpu.CompilerParams(vmem_limit_bytes=VMEM),
        cost_estimate=COST,
        name="deal",
    )(gate, up)


def collect_kernel(places, in_ref, gate_ref, up_ref):
    rows, columns = gate_ref.shape
    piece = columns // (8 * places)
    for which, ref in enumerate((gate_ref, up_ref)):
        pieces = []
        for high in (0, 1):
            for place in range(places):
                for low in (0, 1):
                    for core in (0, 1):
                        start = (4 * which + 2 * high + low) * piece
                        got = in_ref[2 * place + core][:, start : start + piece]
                        pieces.append(got.astype(F32))
        ref[...] = jnp.concatenate(pieces, axis=1)


def collect(places, array):
    _, rows, columns = array.shape
    shape = jax.ShapeDtypeStruct((rows, places * columns), F32)
    return pl.pallas_call(
        functools.partial(collect_kernel, places),
        out_shape=[shape, shape],
        compiler_params=pltpu.CompilerParams(vmem_limit_bytes=VMEM),
        cost_estimate=COST,
        name="collect",
    )(array)


def sum_kernel(count, *refs):
    outs = refs[-count:]
    for at in range(count):
        own, near, relayed = refs[3 * at : 3 * at + 3]
        total = own[...].astype(F32) + near[...].astype(F32) + relayed[...].astype(F32)
        outs[at][...] = total.astype(outs[at].dtype)


def sum_parts(dtype, after, *groups):
    vmem = pl.BlockSpec(memory_space=pltpu.VMEM)
    return pl.pallas_call(
        functools.partial(sum_kernel, len(groups)),
        in_specs=[vmem] * (3 * len(groups)) + [pl.BlockSpec(memory_space=pl.ANY)] * len(after),
        out_shape=[jax.ShapeDtypeStruct(group[0].shape, dtype) for group in groups],
        compiler_params=pltpu.CompilerParams(vmem_limit_bytes=VMEM),
        cost_estimate=COST,
        name="sum_parts",
    )(*[part for group in groups for part in group], *after)


def row_tables(positions, docs):
    inverse = 10000.0 ** (-jnp.arange(0, HEAD_WIDTH, 2).astype(F32) / HEAD_WIDTH)
    angles = positions.astype(F32)[:, None] * inverse[None, :]
    cos, sin = jnp.cos(angles), jnp.sin(angles)
    marks = jnp.stack([positions, docs], axis=1).astype(F32)
    marks = jnp.pad(marks, ((0, 0), (0, 126)))
    return jnp.concatenate([cos] * 4, 1), jnp.concatenate([-sin, sin] * 2, 1), marks


def norm_back(upstream, values, gain):
    scaling = lax.rsqrt(jnp.mean(values * values, axis=-1, keepdims=True) + EPSILON)
    scaled_grad = upstream * gain
    return scaling * scaled_grad - values * (scaling * scaling * scaling) * jnp.mean(
        scaled_grad * values, axis=-1, keepdims=True
    )


class Layout:
    def __init__(self, mesh):
        bits = mesh.shape["ctx"].bit_length() - 1
        self.ctx = tuple(f"p{i}" for i in range(bits))
        self.mesh = Mesh(
            mesh.devices.reshape((2,) * bits + (mesh.shape["fsdp"],)), self.ctx + ("core",)
        )
        self.high, self.low = self.ctx[0], self.ctx[-1]
        self.mid = self.ctx[1:-1]
        self.places = 2 ** len(self.mid)
        self.members = 2 * self.places
        self.all = self.ctx + ("core",)
        self.turn = [
            [(4 * h + 2 * l + c, 4 * c + 2 * (l ^ other) + h) for h in (0, 1) for l in (0, 1) for c in (0, 1)]
            for other in (0, 1)
        ]

    def cross(self, array):
        got = lax.ppermute(array, (self.high, "core"), CROSS)
        return jnp.where(bit(self.high) == bit("core"), array, got)

    def turned(self, array, other, name):
        with jax.named_scope(name):
            return lax.ppermute(array, (self.high, self.low, "core"), self.turn[other])

    def to_team(self, array, name):
        low = bit(self.low)
        return self.turned(pick(array, low), 0, name), self.turned(pick(array, 1 - low), 1, name)

    def in_order(self, blocks):
        both = pair(self.low, *blocks)
        return both.reshape(-1, both.shape[-1])

    def from_team(self, array, name):
        low = bit(self.low)
        both = array.reshape(2, -1, array.shape[-1])
        return pair(
            self.low,
            self.turned(pick(both, low), 0, name),
            self.turned(pick(both, 1 - low), 1, name),
        )

    def team_gather(self, array):
        return lax.all_gather(array, ("core",) + self.mid, axis=0, tiled=True)


    def scatter_cores(self, rows_of, then=None):
        core = bit("core")
        sent = rows_of(1 - core).astype(BF16)
        got = swap(sent, "core", "sum_cores")
        if then is not None:
            then(sent)
        mine = rows_of(core) + got.astype(F32)
        width = mine.shape[1]
        mine = mine.astype(BF16).reshape((2,) * len(self.mid) + (-1, width))
        return [mine[..., : width // 2], mine[..., width // 2 :]]

    def scatter_send(self, parts, count):
        pending = []
        for part, order in zip(parts, (list(self.mid), list(self.mid[::-1]))):
            left = [axis for axis in self.mid if axis not in order[:count]]
            at = left.index(order[count])
            there = bit(order[count])
            pending.append((pick(part, there, at), swap(pick(part, 1 - there, at), order[count], f"sum_places_{count}")))
        return pending

    def scatter_add(self, pending):
        last = pending[0][0].ndim == 2
        parts = [own.astype(F32) + got.astype(F32) for own, got in pending]
        return jnp.concatenate(parts, 1) if last else [part.astype(BF16) for part in parts]

    def scatter_rows(self, rows_of, then=()):
        then = list(then) + [lambda parts: parts] * (1 + len(self.mid) - len(then))
        parts = self.scatter_cores(rows_of, then[0])
        for count in range(len(self.mid)):
            parts = self.scatter_add(self.scatter_send(then[1 + count](parts), count))
        return parts

    def exchange(self, array):
        return lax.all_to_all(array, self.mid + ("core",), 0, 0, tiled=True)

    def rows_out(self, array):
        shape = array.shape
        return jnp.swapaxes(array.reshape((2, self.places) + shape[1:]), 0, 1).reshape(shape)

    def rows_in(self, array):
        shape = array.shape
        return jnp.swapaxes(array.reshape((self.places, 2) + shape[1:]), 0, 1).reshape(shape)


    def start_four(self, array, name):
        return swap(array, self.high, name + "_far"), swap(array, self.low, name + "_near")

    def corner_four(self, far, name):
        return swap(far, self.low, name + "_corner")

    def join_four(self, first, second, own, far, near, corner):
        return pair(first, pair(second, own, near), pair(second, far, corner))

    def relay_sum(self, theirs, got_far, name):
        relay = theirs.astype(F32) + got_far.astype(F32)
        return swap(relay.astype(BF16), self.high, name + "_relay")


def shards(
    layout,
    hidden_in,
    positions,
    doc_ids,
    norm_attn,
    w_query,
    key_weight,
    value_weight,
    w_out,
    norm_mlp,
    w_gate,
    w_up,
    w_down,
    cotangent,
):
    members, places = layout.members, layout.places
    width = hidden_in.shape[-1]
    weight_rows = w_query.shape[0]
    heads = QUERY_HEADS // members
    padded = max(heads, 2)
    query_width = heads * HEAD_WIDTH
    padding = (padded - heads) * HEAD_WIDTH
    tie = lax.optimization_barrier
    place = sum(bit(axis) * 2**at for at, axis in enumerate(layout.mid[::-1]))
    bits = jnp.stack([bit(layout.high), bit(layout.low), 2 * place + bit("core")])
    bits = bits.astype(jnp.int32)
    order = [core * places + place for place in range(places) for core in (0, 1)]
    kv_of = [member * heads // GROUP for member in order]


    blocks = layout.to_team(hidden_in, "hidden")
    docs = layout.cross(pick(doc_ids, bit(layout.low)))
    gains = jnp.stack([norm_attn, norm_mlp], axis=1)
    gains = jnp.pad(gains, ((0, 0), (0, 126)))
    raw = jnp.concatenate([w_query, key_weight, value_weight, gains], axis=1)
    raw_far, raw_near = layout.start_four(raw, "raw")
    x = layout.in_order(blocks)
    x_team = layout.team_gather(x)
    cos, sin, marks = row_tables(positions, docs)
    dealt = deal(places, w_gate, w_up)
    raw_far, raw_near, w_out, cotangent, cos, sin, marks, dealt = tie(
        (raw_far, raw_near, w_out, cotangent, cos, sin, marks, dealt)
    )
    raw_corner = layout.corner_four(raw_far, "raw")
    out_part = layout.cross(w_out)
    g_blocks = layout.to_team(cotangent, "cotangent")
    dealt_attn = deal_attn(
        bits, order, kv_of, query_width, query_width + padding, (raw, raw_far, raw_near, raw_corner)
    )
    dealt_attn, out_part, w_down, *g_blocks = tie((dealt_attn, out_part, w_down, *g_blocks))
    dealt_attn = layout.exchange(dealt_attn)
    down_own = lax.all_gather(w_down, (layout.high, layout.low), axis=0, tiled=True)
    out_far, out_near = layout.start_four(out_part, "out")
    g_rows = layout.in_order(g_blocks)
    g = layout.team_gather(g_rows)
    dealt_attn, out_far, out_near, dealt = tie((dealt_attn, out_far, out_near, dealt))
    dealt = layout.exchange(dealt)
    out_corner = layout.corner_four(out_far, "out")

    normed_attn, q, k, v, kt, vt, gains, w_attn = project(places, x_team, dealt_attn, cos, sin)
    gain_attn, gain_mlp = gains[:1], gains[1:2]
    attended, lse = attend_forward(heads, q, k, vt, marks)
    attended, out_corner, dealt = tie((attended, out_corner, dealt))
    dealt = dealt.reshape(places, 2 * weight_rows, -1)
    chunk = lambda a, at: a[at * places // 2 : (at + 1) * places // 2]
    gu_parts = [chunk(dealt, 0), chunk(dealt, 1)]
    gu_far, gu_near, gu_corner = [None] * 2, [None] * 2, [None] * 2
    gu_far[0], gu_near[0] = layout.start_four(gu_parts[0], "gate_up_0")
    out_own = layout.join_four(layout.low, layout.high, out_part, out_near, out_far, out_corner)
    out_own = out_own.reshape(query_width, width)
    attended = attended[:, :query_width]

    half = x_team.shape[0] // 2
    part = lambda a, core: lax.dynamic_slice_in_dim(a, core * half, half, 0)
    same = lambda parts: parts
    late = {}

    def weights_on(parts):
        *parts, gu_far[0], gu_near[0], gu_parts[1] = tie(
            (*parts, gu_far[0], gu_near[0], gu_parts[1])
        )
        gu_corner[0] = layout.corner_four(gu_far[0], "gate_up_0")
        gu_far[1], gu_near[1] = layout.start_four(gu_parts[1], "gate_up_1")
        return parts

    branch = layout.scatter_rows(lambda core: dot(part(attended, core), out_own))
    (branch,) = weights_on((branch,))
    x_wide = x.astype(F32)
    middle = x_wide + branch
    scale_mlp = lax.rsqrt(jnp.mean(middle * middle, axis=-1, keepdims=True) + EPSILON)
    normed_mlp = layout.team_gather((middle * scale_mlp * gain_mlp).astype(BF16))
    gu_corner[1] = layout.corner_four(gu_far[1], "gate_up_1")

    activated, grad_gu, w_gu = feed_forward(
        bits,
        normed_mlp,
        g,
        down_own,
        [
            parts[at]
            for at in range(2)
            for parts in (gu_parts, gu_far, gu_near, gu_corner)
        ],
    )
    w_gu = w_gu.reshape(width, -1)

    def gu_terms(parts):
        *parts, right = tie((*parts, grad_gu))
        late["theirs"], late["far"] = outer_rows((1,), 2, places, bits, normed_mlp, right)
        return parts

    def gu_others(parts):
        *parts, late["far"], late["theirs"], right = tie(
            (*parts, late["far"], late["theirs"], grad_gu)
        )
        late["far"][0] = swap(late["far"][0], layout.low, "grad_gate_up_far_0")
        late["own"], late["near"] = outer_rows((0,), 2, places, bits, normed_mlp, right)
        return parts

    grad_normed_mlp = layout.scatter_rows(
        lambda core: dot(part(grad_gu, core), w_gu, NT), (None, gu_terms, gu_others)
    )
    gu_theirs, gu_far, gu_own, gu_near = (late[key] for key in ("theirs", "far", "own", "near"))
    grad_normed_mlp, gu_own, gu_near, gu_far[0] = tie((grad_normed_mlp, gu_own, gu_near, gu_far[0]))
    grad_middle = g_rows.astype(F32) + norm_back(grad_normed_mlp, middle, gain_mlp)
    grad_branch = grad_middle.astype(BF16)
    branch_team = layout.team_gather(grad_branch)
    gu_far[0], act, grad_branch, sent = tie((gu_far[0], activated, grad_branch, gu_far[1]))
    gu_relay = [layout.relay_sum(gu_theirs[0], gu_far[0], "grad_gate_up_0")]
    gu_far[1] = swap(sent, layout.low, "grad_gate_up_far_1")
    grad_down = dot(act, g, TN).astype(BF16)
    act, grad_down = tie((act, grad_down))
    final = layout.scatter_cores(lambda core: dot(part(act, core), down_own))
    final = layout.scatter_send(final, 0)
    branch_team, grad_down, gu_far[1], gu_relay[0], gu_near, final = tie(
        (branch_team, grad_down, gu_far[1], gu_relay[0], gu_near, final)
    )
    gu_relay.append(layout.relay_sum(gu_theirs[1], gu_far[1], "grad_gate_up_1"))
    gu_near = [swap(near, layout.low, f"grad_gate_up_near_{at}") for at, near in enumerate(gu_near)]
    grad_down = lax.psum_scatter(
        grad_down, (layout.high, layout.low), scatter_dimension=0, tiled=True
    ).astype(F32)
    for count in range(1, len(layout.mid)):
        final = layout.scatter_send(layout.scatter_add(final), count)
    grad_attended = dot(branch_team, out_own, NT).astype(BF16)
    if padding:
        grad_attended = jnp.pad(grad_attended, ((0, 0), (0, padding)))

    gq, gkv = attend_backward(heads, q, grad_attended, k, v, kt, marks, lse, cos, sin)
    grad_qkv = jnp.concatenate([gq, gkv], axis=1)
    grad_qkv, final, gu_near, gu_relay[1] = tie((grad_qkv, final, gu_near, gu_relay[1]))
    w_attn_own = w_attn.reshape(width, -1)[:, : grad_qkv.shape[1]]

    def attn_terms(sent):
        _, right = tie((sent, grad_qkv))
        late["attn"] = [part for (part,) in outer_rows((1, 0), 1, places, bits, normed_attn, right)]
        late["attn_far"] = swap(late["attn"][1], layout.low, "grad_attn_far")

    def out_terms(parts):
        *parts, late["attn"], right, late["final"] = tie(
            (*parts, late["attn"], branch_team, final)
        )
        late["out"] = outer_quarters(True, bits, attended, right)
        return parts

    def sums_on(parts):
        *parts, late["attn_far"], late["out"], total, own, near, relayed = tie(
            (*parts, late["attn_far"], late["out"], late["final"], gu_own, gu_near, gu_relay)
        )
        late["total"] = (middle + layout.scatter_add(total)).astype(BF16)
        late["attn_relay"] = layout.relay_sum(late["attn"][0], late["attn_far"], "grad_attn")
        late["out_far"] = swap(late["out"][3], layout.low, "grad_out_far")
        late["gate_up"] = sum_parts(BF16, (parts[0],), *zip(own, near, relayed))
        return parts

    grad_normed_attn = layout.scatter_rows(
        lambda core: dot(part(grad_qkv, core), w_attn_own, NT), (attn_terms, out_terms, sums_on)
    )
    attn_parts, out_parts = late["attn"], late["out"]
    grad_normed_attn, out_far, attn_sent, gu_sums = tie(
        (grad_normed_attn, late["out_far"], attn_parts[3], late["gate_up"])
    )
    grad_normed_attn, grad_down = tie((grad_normed_attn, grad_down))
    attn_relay = late["attn_relay"]
    attn_near = swap(attn_sent, layout.low, "grad_attn_near")
    out_relay = layout.relay_sum(out_parts[2], out_far, "grad_out")
    out_near = swap(out_parts[1], layout.low, "grad_out_near")
    grad_input = grad_middle + norm_back(grad_normed_attn, x_wide, gain_attn)
    grad_rows = grad_input.astype(BF16)
    home = layout.from_team(jnp.concatenate([late["total"], grad_rows], axis=1), "rows_home")
    block_out, grad_input = home[..., :width], home[..., width:].astype(F32)

    by_member = lambda a: a.reshape(members, weight_rows, -1)
    dealt = layout.exchange(by_member(jnp.concatenate(gu_sums)))
    (grad_attn,) = sum_parts(BF16, (grad_rows, dealt), (attn_parts[2], attn_near, attn_relay))
    grad_attn = layout.rows_in(layout.exchange(by_member(grad_attn))).astype(F32)
    (grad_out,) = sum_parts(BF16, (grad_rows,), (out_parts[0], out_near, out_relay))
    grad_out = layout.cross(grad_out).astype(F32)
    grad_gate, grad_up = collect(places, dealt)

    def sum_kv(array):
        return array.reshape((KEY_VALUE_HEADS, -1) + array.shape[1:]).sum(1)

    def lay(array):
        return jnp.swapaxes(array, 0, 1).reshape(array.shape[1], -1)

    grad_query = lay(grad_attn[:, :, :query_width])
    grad_kv = sum_kv(grad_attn[:, :, query_width + padding :])
    grad_key = lay(grad_kv[:, :, :HEAD_WIDTH])
    grad_value = lay(grad_kv[:, :, HEAD_WIDTH:])

    def gain_gradient(gain, *terms):
        total = sum(jnp.sum(w.astype(F32) * grad, axis=1) for w, grad in terms)
        return total / gain.astype(F32)

    grad_norm_attn = gain_gradient(
        norm_attn, (w_query, grad_query), (key_weight, grad_key), (value_weight, grad_value)
    )
    grad_norm_mlp = gain_gradient(norm_mlp, (w_gate, grad_gate), (w_up, grad_up))

    return (
        block_out,
        grad_input,
        grad_norm_attn,
        grad_query,
        grad_key,
        grad_value,
        grad_out,
        grad_norm_mlp,
        grad_gate,
        grad_up,
        grad_down,
    )


def solution(mesh):
    layout = Layout(mesh)
    tokens = P("core", layout.ctx, None)
    rows = P(layout.all, None)
    line = P(layout.all)
    in_specs = (
        tokens, P(), P("core", None), line, rows, rows, rows, rows, line, rows, rows, rows, tokens,
    )
    out_specs = (tokens, tokens, line, rows, rows, rows, rows, line, rows, rows, rows)
    return jax.shard_map(
        functools.partial(shards, layout),
        mesh=layout.mesh,
        in_specs=in_specs,
        out_specs=out_specs,
        check_vma=False,
    )
```
